256 devices in a mesh: store: 64 (over z, y, core), tp: 4 (over x).
Axes of the slice: x: 4, y: 4, z: 8, core: 2. Of those that a mesh axis runs over, the one named last changes fastest.
Arguments:
- slot_anchor: bfloat16 [81920, 8, 256], P(('store', 'tp')), may hold values from -6 to 6
- slot_delta: bfloat16 [81920, 4, 8, 256], P(('store', 'tp')), may hold values from -6 to 6
- slot_scale: bfloat16 [81920, 8, 2], P(('store', 'tp')), may hold values from 0.25 to 1
- send_slot: int32 [256, 64, 5], P(('store', 'tp')), may hold values from -1 to 319, as said below
- recv_block: int32 [64, 256, 5], P('store'), may hold values from -1 to 1023, as said below
- turn_queries: bfloat16 [8192, 8, 1024], P(('store', 'tp')), may hold values from -28 to 28
- turn_kv: bfloat16 [8192, 8, 256], P(('store', 'tp')), may hold values from -9 to 9
Outputs:
- cache_out: bfloat16 [64, 4224, 8, 256], P('store', None, 'tp')
- attended: bfloat16 [8192, 8, 1024], P(('store', 'tp'))
The draws below stay inside these ranges and needn't reach their ends.
Inputs may be any that keep to these rules, and one draw needn't show every extreme that they name: Holder g sends its slot send_slot[g, o, c] as place c to session o, -1 for none; no slot of a holder is named twice; for each holder and session the named places come first; at most 5 named places for one holder and one session, and every session has some holder with 5. recv_block[o, g, c] is -1 exactly where send_slot[g, o, c] is -1; every block 0 to 1023 of a session is named exactly once.
All inputs are finite; a program needn't handle non-finite values.
Results may differ from the reference program's by a relative error of at most 0.0082.
Values may be sent and summed in bfloat16 or wider, within the bound.
A program may use at most 128 MiB of HBM per device.

```python
import math
import jax
import jax.numpy as jnp
from jax import lax

KVH = 8
QPG = 8
HD = 128
BLK = 4
CTX = 4096
TURN = 128
SESSIONS = 64
HOLDERS = 256
NBLK = 1024
CAP = 5
HOLD = 320


def plan_tables(key):
    holder_total = HOLDERS
    sub_keys = jax.random.split(key, 3)
    forced = jax.random.randint(sub_keys[0], (SESSIONS,), 0, holder_total)
    positions = jnp.arange(holder_total * CAP, dtype=jnp.int32)
    position_holder = positions // CAP

    def one_owner(owner_key, forced_holder):
        order_key, block_key = jax.random.split(owner_key)
        shuffled = jax.random.permutation(order_key, holder_total * CAP).astype(jnp.int32)
        ranking = jnp.where(position_holder == forced_holder, positions - holder_total * CAP, shuffled)
        picked = jnp.argsort(ranking)[:NBLK]
        chosen = jnp.zeros((holder_total * CAP,), jnp.int32).at[picked].set(1)
        counts = chosen.reshape(holder_total, CAP).sum(axis=1)
        live_flags = (jnp.arange(CAP, dtype=jnp.int32)[None, :] < counts[:, None]).reshape(-1)
        live_rank = jnp.cumsum(live_flags.astype(jnp.int32)) - 1
        blocks = jax.random.permutation(block_key, NBLK).astype(jnp.int32)
        named = jnp.where(live_flags, blocks[jnp.clip(live_rank, 0, NBLK - 1)], -1)
        return named.reshape(holder_total, CAP).astype(jnp.int32)
    received = jax.vmap(one_owner)(jax.random.split(sub_keys[1], SESSIONS), forced)
    slot_orders = jax.vmap(lambda slot_key: jax.random.permutation(slot_key, SESSIONS * CAP))(jax.random.split(sub_keys[2], holder_total)).astype(jnp.int32)
    base_slots = (jnp.arange(SESSIONS)[:, None] * CAP + jnp.arange(CAP)[None, :]).reshape(-1)
    sent_slots = slot_orders[:, base_slots].reshape(holder_total, SESSIONS, CAP)
    sent_slots = jnp.where(jnp.transpose(received, (1, 0, 2)) >= 0, sent_slots, -1).astype(jnp.int32)
    return (received, sent_slots)


def turn_tables(key):
    sub_keys = jax.random.split(key, 3)
    rows = SESSIONS * TURN
    query_base = jnp.clip(jax.random.normal(sub_keys[0], (rows, KVH, QPG * HD), jnp.float32), -6.0, 6.0)
    pair_base = jnp.clip(jax.random.normal(sub_keys[2], (rows, KVH, 2 * HD), jnp.float32), -6.0, 6.0)
    queries = 2.5 * query_base
    pairs = 1.5 * pair_base
    key_part = pairs[..., :HD]
    pairs = jnp.concatenate([key_part, pairs[..., HD:]], axis=-1)
    return (queries, pairs)


def draw_send_slot(key, part):
    received, sent_slots = plan_tables(key)
    return sent_slots


def draw_recv_block(key, part):
    received, sent_slots = plan_tables(key)
    return received


def draw_turn_queries(key, part):
    queries, pairs = turn_tables(key)
    return queries.astype(jnp.bfloat16)


def draw_turn_kv(key, part):
    queries, pairs = turn_tables(key)
    return pairs.astype(jnp.bfloat16)


def levels(stream_key, shape, cuts, low, top_value):
    factor_of = 1.0
    for position, shards_of in cuts:
        draws = jax.random.uniform(jax.random.fold_in(jax.random.fold_in(stream_key, 6), position), (shards_of,), jnp.float32, low / len(cuts), top_value / len(cuts))
        factor_of = factor_of * jnp.repeat(jnp.exp(draws), shape[position] // shards_of).reshape((-1,) + (1,) * (len(shape) - 1 - position))
    return factor_of


def gaussian(own_key, extent, scale, most, pieces=(), held_as=jnp.bfloat16):
    drawn = scale * jax.random.normal(own_key, extent, jnp.float32)
    if pieces:
        drawn = drawn * levels(own_key, extent, pieces, -0.22, 0.18)
    return jnp.clip(drawn, -most, most).astype(held_as)


def setup_inputs(seed: int = 0) -> dict:
    splits = jax.random.split(jax.random.key(seed), 8)
    slot_anchor = gaussian(splits[0], (HOLDERS * HOLD, KVH, 2 * HD), 0.8, 6.0, ((0, 256),))
    slot_delta = gaussian(splits[1], (HOLDERS * HOLD, BLK, KVH, 2 * HD), 1.0, 6.0, ((0, 256),))
    slot_scale = jnp.clip(jnp.exp(math.log(1.0) - 1.3862944 * jax.random.uniform(splits[2], (HOLDERS * HOLD, KVH, 2), jnp.float32) ** levels(splits[2], (HOLDERS * HOLD, KVH, 2), ((0, 256),), -0.2, 0.2)), 0.25, 1.0).astype(jnp.bfloat16)
    send_slot = draw_send_slot(jax.random.fold_in(splits[7], 71), 0)
    recv_block = draw_recv_block(jax.random.fold_in(splits[7], 71), 0)
    turn_queries = draw_turn_queries(jax.random.fold_in(splits[7], 71), 0)
    turn_kv = draw_turn_kv(jax.random.fold_in(splits[7], 71), 0)
    return dict(slot_anchor=slot_anchor, slot_delta=slot_delta, slot_scale=slot_scale, send_slot=send_slot, recv_block=recv_block, turn_queries=turn_queries, turn_kv=turn_kv)


def decode_rows(anchors, deltas, scales):
    head_size = deltas.shape[-1] // 2
    spread = jnp.repeat(scales.astype(jnp.float32), head_size, axis=-1)
    return (anchors.astype(jnp.float32) + spread * deltas.astype(jnp.float32)).astype(jnp.bfloat16)

def attend(queries, restored, context):
    head_size = restored.shape[-1] // 2
    turn_length = queries.shape[0]
    groups = restored.shape[1]
    query_heads = queries.reshape(turn_length, groups, -1, head_size).astype(jnp.float32)
    key_rows = restored[..., :head_size].astype(jnp.float32)
    values = restored[..., head_size:].astype(jnp.float32)
    scores = jnp.einsum('tkgd,skd->kgts', query_heads, key_rows) * (1.0 / math.sqrt(head_size))
    allowed = jnp.arange(restored.shape[0])[None, :] < context + 1 + jnp.arange(turn_length)[:, None]
    scores = jnp.where(allowed, scores, -jnp.inf)
    row_max = lax.optimization_barrier(jnp.max(scores, axis=-1, keepdims=True))
    powers = jnp.exp(scores - row_max)
    row_total = lax.optimization_barrier(jnp.sum(powers, axis=-1, keepdims=True))
    weights = (powers / row_total).astype(jnp.bfloat16)
    mixture = jnp.einsum('kgts,skd->tkgd', weights.astype(jnp.float32), values)
    return mixture.astype(jnp.bfloat16).reshape(turn_length, groups, -1)

def reference(slot_anchor, slot_delta, slot_scale, send_slot, recv_block, turn_queries, turn_kv):
    holders = send_slot.shape[0]
    slot_count = slot_anchor.shape[0] // holders
    anchors = slot_anchor.reshape((holders, slot_count) + slot_anchor.shape[1:])
    deltas = slot_delta.reshape((holders, slot_count) + slot_delta.shape[1:])
    scales = slot_scale.reshape((holders, slot_count) + slot_scale.shape[1:])
    holder_rows = jnp.arange(holders, dtype=jnp.int32)[:, None]

    def restore(owner_index):
        slot_index = send_slot[:, owner_index, :]
        safe_slot = jnp.maximum(slot_index, 0)
        decoded = decode_rows(anchors[holder_rows, safe_slot][:, :, None], deltas[holder_rows, safe_slot], scales[holder_rows, safe_slot][:, :, None])
        block_ids = recv_block[owner_index]
        target = jnp.where(block_ids >= 0, block_ids, NBLK)
        cache_rows = jnp.zeros((NBLK,) + decoded.shape[2:], jnp.bfloat16).at[target].set(decoded, mode='drop')
        turn_rows = lax.dynamic_slice_in_dim(turn_kv, owner_index * TURN, TURN, 0)
        restored = jnp.concatenate([cache_rows.reshape((CTX,) + decoded.shape[3:]), turn_rows], axis=0)
        queries = lax.dynamic_slice_in_dim(turn_queries, owner_index * TURN, TURN, 0)
        return (restored, attend(queries, restored, CTX))
    caches, outputs = lax.map(restore, jnp.arange(SESSIONS, dtype=jnp.int32))
    return (caches, outputs.reshape(SESSIONS * TURN, KVH, QPG * HD))
```

```python
import math

import jax
import jax.numpy as jnp
from jax import lax
from jax.experimental import pallas as pl
from jax.experimental.pallas import tpu as pltpu
from jax.sharding import PartitionSpec as P

MESH = pl.DeviceIdType.MESH
NZ, NY, NC, NX = 8, 4, 2, 4
PLANES = NY * NC
PER_STEP = NZ * NX
CAP = 5
BLK = 4
HD = 128
QPG = 8
NBLK = 1024
TOK = 32
TURN = TOK * NX
HEADS = 2
ROWS = QPG * TOK
KEYS = PER_STEP * CAP * BLK
TURN_TILES = TURN // BLK
SCALE2 = math.log2(math.e) / math.sqrt(HD)
LOW = -1e30


def body(
    anchor_hbm, delta_hbm, scale_ref, slot_ref, inv_ref, bias_ref, q_hbm, kv_hbm,
    cache_hbm, att_hbm,
    anchor_v, delta_v, q_v, kv_v, att_v,
    perm, qf, qsend, qarr, kvsend, kvarr, send, arr,
    flat, keys, values, acc, top, outsend, outarr, stage,
    load_sem, send_sem, recv_sem, turn_send, turn_recv, back_send, back_recv, store_sem,
):
    store = lax.axis_index("store")
    x = lax.axis_index("tp")
    z, y, core = store // (NY * NC), (store // NC) % NY, store % NC

    loads = [
        pltpu.make_async_copy(src, dst, load_sem.at[i])
        for i, (src, dst) in enumerate(
            ((q_hbm, q_v), (kv_hbm, kv_v), (anchor_hbm, anchor_v), (delta_hbm, delta_v))
        )
    ]
    for load in loads:
        load.start()

    barrier = pltpu.get_barrier_semaphore()

    def greet(i, _):
        other = lax.rem(store * NX + x + 1 + i, NZ * NY * NC * NX)
        pl.semaphore_signal(
            barrier, inc=1, device_id=(other // NX, other % NX), device_id_type=MESH
        )
        return 0

    lax.fori_loop(0, NZ * NY * NC * NX - 1, greet, 0)

    out_row = lax.broadcasted_iota(jnp.int32, (64, 64), 0)
    in_row = lax.broadcasted_iota(jnp.int32, (64, 64), 1)
    wanted = ((out_row >> 1) & 7) * 8 + (out_row >> 4) * 2 + (out_row & 1)
    perm[...] = jnp.where(in_row == wanted, 1.0, 0.0).astype(jnp.bfloat16)

    def split(tiles):
        wide = jnp.concatenate(tiles, axis=1).astype(jnp.bfloat16)
        return jnp.dot(perm[...], wide, preferred_element_type=jnp.float32).astype(jnp.bfloat16)

    loads[0].wait()
    for q in range(QPG):
        lanes = q_v[:, :, q * HD : (q + 1) * HD].astype(jnp.float32)
        qf[q] = lanes.reshape(TOK * 8, HD)
        for h in range(8):
            rows = qf[q, pl.ds(h, TOK, stride=8), :]
            qsend[h // 2, h % 2, q * TOK : (q + 1) * TOK, :] = rows.astype(jnp.bfloat16)
    loads[1].wait()
    turn_blocks = []
    for b in range(TOK // BLK):
        parts = []
        for r in range(BLK):
            row = kv_v[b * BLK + r].astype(jnp.float32)
            parts += [row[:, :HD], row[:, HD:]]
        turn_blocks.append(jnp.concatenate(parts, axis=0))
    mixed = split(turn_blocks)
    for t in range(NX):
        for b in range(TOK // BLK):
            kvsend[t, b] = mixed[t * 16 : (t + 1) * 16, b * HD : (b + 1) * HD]

    pl.semaphore_wait(barrier, NZ * NY * NC * NX - 1)

    def turn_copies(d):
        to = lax.rem(x + d, NX)
        return (
            pltpu.make_async_remote_copy(
                qsend.at[to], qarr.at[x], turn_send.at[0, d - 1], turn_recv.at[0, d - 1],
                device_id=(store, to), device_id_type=MESH,
            ),
            pltpu.make_async_remote_copy(
                kvsend.at[to], kvarr.at[x], turn_send.at[1, d - 1], turn_recv.at[1, d - 1],
                device_id=(store, to), device_id_type=MESH,
            ),
        )

    for d in range(1, NX):
        for copy in turn_copies(d):
            copy.start()
    qarr[x] = qsend[x]
    kvarr[x] = kvsend[x]

    loads[2].wait()
    loads[3].wait()

    def send_session(k, _):
        j, i = k // NZ, k % NZ
        half = i // 2 + 1
        dz = jnp.where(i == NZ - 1, 0, jnp.where(i % 2 == 0, half, NZ - half))
        z2, y2 = lax.rem(z + dz, NZ), lax.rem(y + j // NC, NY)
        core2 = lax.rem(core + j % NC, NC)
        session = (z2 * NY + y2) * NC + core2
        tiles = []
        for c in range(CAP):
            slot = slot_ref[session * CAP + c]
            scale = scale_ref[slot].astype(jnp.float32)
            anchor = anchor_v[slot].astype(jnp.float32)
            parts = []
            for r in range(BLK):
                delta = delta_v[slot, r].astype(jnp.float32)
                parts.append(anchor[:, :HD] + scale[:, 0:1] * delta[:, :HD])
                parts.append(anchor[:, HD:] + scale[:, 1:2] * delta[:, HD:])
            tiles.append(jnp.concatenate(parts, axis=0))
        mixed = split(tiles)
        for t in range(NX):
            for c in range(CAP):
                send[k, t, c] = mixed[t * 16 : (t + 1) * 16, c * HD : (c + 1) * HD]
        mine = (core * 1 + y * NC) * PER_STEP + z * NX + x
        for d in range(NX):
            to = lax.rem(x + d, NX)
            copy = pltpu.make_async_remote_copy(
                send.at[k, to], arr.at[mine], send_sem.at[j], recv_sem.at[j],
                device_id=(session, to), device_id_type=MESH,
            )
            if d:
                copy.start()
            else:
                pl.when(k != NZ - 1)(copy.start)

        @pl.when(k == NZ - 1)
        def _():
            arr[mine] = send[NZ - 1, x]

        return 0

    lax.fori_loop(0, PLANES * NZ, send_session, 0)

    for d in range(1, NX):
        for copy in turn_copies(d):
            copy.wait()

    ones = jnp.ones((KEYS, HD), jnp.bfloat16)
    values[0, :, HD:] = ones
    values[1, :, HD:] = ones

    def unpack(tiles, count):
        flat[pl.ds(0, count * 4), :] = tiles.astype(jnp.float32).reshape(count * 4, HD)
        for h in range(HEADS):
            keys[h, pl.ds(0, count), :] = flat[pl.ds(h, count, stride=4), :].astype(jnp.bfloat16)
            values[h, pl.ds(0, count), :HD] = flat[pl.ds(2 + h, count, stride=4), :].astype(
                jnp.bfloat16
            )

    unpack(kvarr[...].reshape(TURN_TILES, 16, HD), TURN)
    token = lax.broadcasted_iota(jnp.int32, (ROWS, TURN), 0) & (TOK - 1)
    position = lax.broadcasted_iota(jnp.int32, (ROWS, TURN), 1)
    for h in range(HEADS):
        for g in range(NX):
            scores = lax.dot_general(
                qarr[g, h], keys[h, :TURN, :], (((1,), (1,)), ((), ())),
                preferred_element_type=jnp.float32,
            )
            scores = jnp.where(position <= token + g * TOK, scores * SCALE2, LOW)
            peak = jnp.max(scores, axis=1, keepdims=True)
            power = jnp.exp2(scores - peak).astype(jnp.bfloat16)
            acc[h, g] = jnp.dot(power, values[h, :TURN, :], preferred_element_type=jnp.float32)
            top[h, g] = jnp.broadcast_to(peak, (ROWS, HD))

    def attend(j, _):
        source = lax.rem(y + NY - j // NC, NY) * NC + lax.rem(core + NC - j % NC, NC)
        first = source * PER_STEP

        def arrived(count):
            span = arr.at[pl.ds(first, count)]
            pltpu.make_async_remote_copy(
                span, span, send_sem.at[j], recv_sem.at[j],
                device_id=(store, lax.rem(x + 1, NX)), device_id_type=MESH,
            ).wait_recv()

        @pl.when(j == 0)
        def _():
            arrived(PER_STEP - 1)

        @pl.when(j != 0)
        def _():
            arrived(PER_STEP)

        unpack(arr[pl.ds(first, PER_STEP)].reshape(PER_STEP * CAP, 16, HD), KEYS)
        bias = bias_ref[source]
        for h in range(HEADS):
            for g in range(NX):
                scores = lax.dot_general(
                    qarr[g, h], keys[h], (((1,), (1,)), ((), ())),
                    preferred_element_type=jnp.float32,
                )
                scores = scores * SCALE2 + bias
                before = top[h, g][:, 0:1]
                peak = jnp.maximum(before, jnp.max(scores, axis=1, keepdims=True))
                power = jnp.exp2(scores - peak).astype(jnp.bfloat16)
                acc[h, g] = acc[h, g] * jnp.exp2(before - peak) + jnp.dot(
                    power, values[h], preferred_element_type=jnp.float32
                )
                top[h, g] = jnp.broadcast_to(peak, (ROWS, HD))
        return 0

    lax.fori_loop(0, PLANES, attend, 0)

    def back_copy(d):
        to = lax.rem(x + d, NX)
        return pltpu.make_async_remote_copy(
            outsend.at[to], outarr.at[x], back_send.at[d - 1], back_recv.at[d - 1],
            device_id=(store, to), device_id_type=MESH,
        )

    for d in (2, 1, 3, 0):
        g = lax.rem(x + d, NX)
        for h in range(HEADS):
            total = acc[h, g]
            outsend[g, h] = (total[:, :HD] / total[:, HD:]).astype(jnp.bfloat16)
        if d:
            back_copy(d).start()
        else:
            outarr[x] = outsend[x]

    def place(b, _):
        stage[b] = arr[inv_ref[b] // CAP, inv_ref[b] % CAP]
        return 0

    lax.fori_loop(0, NBLK, place, 0, unroll=8)
    stage[NBLK:] = kvarr[...].reshape(TURN_TILES, 16, HD)
    cache_copy = pltpu.make_async_copy(stage, cache_hbm, store_sem.at[0])
    cache_copy.start()

    for d in range(1, NX):
        back_copy(d).wait()
    for t in range(NX):
        for hh in range(HEADS):
            for q in range(QPG):
                qf[q, pl.ds(t * 2 + hh, TOK, stride=8), :] = outarr[
                    t, hh, q * TOK : (q + 1) * TOK, :
                ].astype(jnp.float32)
    for q in range(QPG):
        att_v[:, :, q * HD : (q + 1) * HD] = qf[q].reshape(TOK, 8, HD).astype(jnp.bfloat16)
    att_copy = pltpu.make_async_copy(att_v, att_hbm, store_sem.at[1])
    att_copy.start()

    for j in range(PLANES):
        count = PER_STEP - 1 if j == 0 else PER_STEP
        span = arr.at[pl.ds(j * PER_STEP, count)]
        pltpu.make_async_remote_copy(
            span, span, send_sem.at[j], recv_sem.at[j],
            device_id=(store, lax.rem(x + 1, NX)), device_id_type=MESH,
        ).wait_send()
    cache_copy.wait()
    att_copy.wait()


def shards(slot_anchor, slot_delta, slot_scale, send_slot, recv_block, turn_queries, turn_kv):
    slots = jnp.maximum(send_slot, 0).reshape(-1)
    planned = recv_block[0].reshape(NZ, PLANES, NX, CAP).transpose(1, 0, 2, 3)
    bias = jnp.where(planned >= 0, 0.0, LOW).astype(jnp.float32)
    bias = jnp.repeat(bias.reshape(PLANES, 1, PER_STEP * CAP), BLK, axis=2)
    places = planned.reshape(-1, 1)
    hits = places == jnp.arange(NBLK)[None, :]
    inverse = jnp.sum(jnp.where(hits, jnp.arange(NBLK + 256)[:, None], 0), axis=0)
    bf16, f32 = jnp.bfloat16, jnp.float32
    cache, attended = pl.pallas_call(
        body,
        out_shape=(
            jax.ShapeDtypeStruct((NBLK + TURN_TILES, 16, HD), bf16),
            jax.ShapeDtypeStruct((TOK, 8, QPG * HD), bf16),
        ),
        in_specs=[
            pl.BlockSpec(memory_space=pl.ANY),
            pl.BlockSpec(memory_space=pl.ANY),
            pl.BlockSpec(memory_space=pltpu.VMEM),
            pl.BlockSpec(memory_space=pltpu.SMEM),
            pl.BlockSpec(memory_space=pltpu.SMEM),
            pl.BlockSpec(memory_space=pltpu.VMEM),
            pl.BlockSpec(memory_space=pl.ANY),
            pl.BlockSpec(memory_space=pl.ANY),
        ],
        out_specs=(pl.BlockSpec(memory_space=pl.ANY), pl.BlockSpec(memory_space=pl.ANY)),
        scratch_shapes=[
            pltpu.VMEM(slot_anchor.shape, bf16),
            pltpu.VMEM(slot_delta.shape, bf16),
            pltpu.VMEM(turn_queries.shape, bf16),
            pltpu.VMEM(turn_kv.shape, bf16),
            pltpu.VMEM(turn_queries.shape, bf16),
            pltpu.VMEM((64, 64), bf16),
            pltpu.VMEM((QPG, TOK * 8, HD), f32),
            pltpu.VMEM((NX, HEADS, ROWS, HD), bf16),
            pltpu.VMEM((NX, HEADS, ROWS, HD), bf16),
            pltpu.VMEM((NX, TOK // BLK, 16, HD), bf16),
            pltpu.VMEM((NX, TOK // BLK, 16, HD), bf16),
            pltpu.VMEM((PLANES * NZ, NX, CAP, 16, HD), bf16),
            pltpu.VMEM((PLANES * PER_STEP, CAP, 16, HD), bf16),
            pltpu.VMEM((KEYS * 4, HD), f32),
            pltpu.VMEM((HEADS, KEYS, HD), bf16),
            pltpu.VMEM((HEADS, KEYS, 2 * HD), bf16),
            pltpu.VMEM((HEADS, NX, ROWS, 2 * HD), f32),
            pltpu.VMEM((HEADS, NX, ROWS, HD), f32),
            pltpu.VMEM((NX, HEADS, ROWS, HD), bf16),
            pltpu.VMEM((NX, HEADS, ROWS, HD), bf16),
            pltpu.VMEM((NBLK + TURN_TILES, 16, HD), bf16),
            pltpu.SemaphoreType.DMA((4,)),
            pltpu.SemaphoreType.DMA((PLANES,)),
            pltpu.SemaphoreType.DMA((PLANES,)),
            pltpu.SemaphoreType.DMA((2, NX - 1)),
            pltpu.SemaphoreType.DMA((2, NX - 1)),
            pltpu.SemaphoreType.DMA((NX - 1,)),
            pltpu.SemaphoreType.DMA((NX - 1,)),
            pltpu.SemaphoreType.DMA((2,)),
        ],
        compiler_params=pltpu.CompilerParams(
            collective_id=0, has_side_effects=True, vmem_limit_bytes=48 * 2**20
        ),
        name="restore_attend",
    )(
        slot_anchor, slot_delta, slot_scale, slots, inverse, bias, turn_queries, turn_kv
    )
    cache = cache.reshape(NBLK + TURN_TILES, BLK, 2, HEADS, HD).transpose(0, 1, 3, 2, 4)
    return cache.reshape(1, (NBLK + TURN_TILES) * BLK, HEADS, 2 * HD), attended


def solution(mesh):
    placed = (
        P(("store", "tp"), None, None),
        P(("store", "tp"), None, None, None),
        P(("store", "tp"), None, None),
        P(("store", "tp"), None, None),
        P("store", None, None),
        P(("store", "tp"), None, None),
        P(("store", "tp"), None, None),
    )
    return jax.shard_map(
        shards,
        mesh=mesh,
        in_specs=placed,
        out_specs=(P("store", None, "tp", None), P(("store", "tp"), None, None)),
        check_vma=False,
    )
```

```python
import math

import jax
import jax.numpy as jnp
from jax import lax
from jax.experimental import pallas as pl
from jax.experimental.pallas import tpu as pltpu
from jax.sharding import PartitionSpec as P

MESH = pl.DeviceIdType.MESH
NZ, NY, NC, NX = 8, 4, 2, 4
PLANES = NY * NC
PER_STEP = NZ * NX
CAP = 5
BLK = 4
HD = 128
QPG = 8
NBLK = 1024
TOK = 32
TURN = TOK * NX
HEADS = 2
ROWS = QPG * TOK
KEYS = PER_STEP * CAP * BLK
TURN_TILES = TURN // BLK
SCALE2 = math.log2(math.e) / math.sqrt(HD)
LOW = -1e30
Y_STEPS = sum(d << (2 * i) for i, d in enumerate((2, 2, 1, 3, 1, 3, 0, 0)))
C_STEPS = sum(d << i for i, d in enumerate((0, 1, 0, 1, 1, 0, 1, 0)))
Z_ORDER = (4, 3, 5, 0, 2, 6, 1, 7)
Z_STEPS = sum(d << (3 * i) for i, d in enumerate(Z_ORDER))
SELF = (PLANES - 1) * NZ + Z_ORDER.index(0)
PIECES = 8
VMEM = 62148608


def body(
    anchor_hbm, delta_hbm, scale_hbm, slot_hbm, recv_hbm, q_hbm, kv_hbm,
    cache_out, att_v,
    anchor_v, delta_v, scale_v, slot_ref, recv_ref, q_v, kv_v, stage, spread, bias_v, inv_v, inv_ref,
    perm, qf, qsend, qarr, kvsend, kvarr, send, arr,
    flat, keys, values, acc, top, outsend, outarr,
    load_sem, send_sem, recv_sem, turn_send, turn_recv, back_send, back_recv, inv_sem, out_sem,
):
    store = lax.axis_index("store")
    x = lax.axis_index("tp")
    z, y, core = store // (NY * NC), (store // NC) % NY, store % NC

    loads = [
        pltpu.make_async_copy(src, dst, load_sem.at[i])
        for i, (src, dst) in enumerate(
            (
                (q_hbm, q_v), (kv_hbm, kv_v), (scale_hbm, scale_v), (slot_hbm, slot_ref),
                (recv_hbm, recv_ref), (anchor_hbm, anchor_v), (delta_hbm, delta_v),
            )
        )
    ]
    for load in loads:
        load.start()

    barrier = pltpu.get_barrier_semaphore()

    me = store * NX + x
    devices = NZ * NY * NC * NX

    def greet(i, _):
        other = (me + 1 + i) & (devices - 1)
        pl.semaphore_signal(
            barrier, inc=1, device_id=(other >> 2, other & 3), device_id_type=MESH
        )
        return 0

    lax.fori_loop(0, devices - 1, greet, 0, unroll=15)

    out_row = lax.broadcasted_iota(jnp.int32, (64, 64), 0)
    in_row = lax.broadcasted_iota(jnp.int32, (64, 64), 1)
    wanted = ((out_row >> 1) & 7) * 8 + (out_row >> 4) * 2 + (out_row & 1)
    perm[...] = jnp.where(in_row == wanted, 1.0, 0.0).astype(jnp.bfloat16)

    def split(tiles):
        wide = jnp.concatenate(tiles, axis=1).astype(jnp.bfloat16)
        return jnp.dot(perm[...], wide, preferred_element_type=jnp.float32).astype(jnp.bfloat16)

    loads[2].wait()
    scale = scale_v[...].astype(jnp.float32)
    slots = scale.shape[2]
    for kv in range(2):
        flat[kv * 8 : kv * 8 + 8, :] = scale[:, kv, :HD]
        flat[16 + kv * 8 : 24 + kv * 8, :] = scale[:, kv, HD : 2 * HD]
        flat[32 + kv * 8 : 40 + kv * 8, : slots - 2 * HD] = scale[:, kv, 2 * HD :]
    for slot in range(slots):
        part, lane = slot // HD * 16, slot % HD
        for kv in range(2):
            column = flat[part + kv * 8 : part + kv * 8 + 8, lane : lane + 1]
            spread[kv, slot] = jnp.broadcast_to(column, (8, HD))

    loads[0].wait()
    for q in range(QPG):
        lanes = q_v[:, :, q * HD : (q + 1) * HD].astype(jnp.float32)
        qf[q] = lanes.reshape(TOK * 8, HD)
        for h in range(8):
            rows = qf[q, pl.ds(h, TOK, stride=8), :]
            qsend[h // 2, h % 2, q * TOK : (q + 1) * TOK, :] = rows.astype(jnp.bfloat16)
    loads[1].wait()
    turn_blocks = []
    for b in range(TOK // BLK):
        parts = []
        for r in range(BLK):
            row = kv_v[b * BLK + r].astype(jnp.float32)
            parts += [row[:, :HD], row[:, HD:]]
        turn_blocks.append(jnp.concatenate(parts, axis=0))
    mixed = split(turn_blocks)
    for t in range(NX):
        for b in range(TOK // BLK):
            kvsend[t, b] = mixed[t * 16 : (t + 1) * 16, b * HD : (b + 1) * HD]

    pl.semaphore_wait(barrier, devices - 1)

    def turn_copies(d):
        to = lax.rem(x + d, NX)
        return (
            pltpu.make_async_remote_copy(
                qsend.at[to], qarr.at[x], turn_send.at[0, d - 1], turn_recv.at[0, d - 1],
                device_id=(store, to), device_id_type=MESH,
            ),
            pltpu.make_async_remote_copy(
                kvsend.at[to], kvarr.at[x], turn_send.at[1, d - 1], turn_recv.at[1, d - 1],
                device_id=(store, to), device_id_type=MESH,
            ),
        )

    for load in loads[3:]:
        load.wait()

    def offsets(j):
        return (Y_STEPS >> (2 * j)) & (NY - 1), (C_STEPS >> j) & (NC - 1)

    def z_offset(i):
        return (Z_STEPS >> (3 * i)) & (NZ - 1)

    def send_session(k, _):
        j, i = k >> 3, k & 7
        dy, dc = offsets(j)
        z2, y2, core2 = (z + z_offset(i)) & (NZ - 1), (y + dy) & (NY - 1), (core + dc) & (NC - 1)
        session = (z2 * NY + y2) * NC + core2
        box = j + jnp.where(k >= (PLANES - 1) * NZ + NZ // 2, 1, 0)
        tiles = []
        for c in range(CAP):
            slot = jnp.maximum(slot_ref[c, 0, session], 0)
            key_scale, value_scale = spread[0, slot], spread[1, slot]
            anchor = anchor_v[slot].astype(jnp.float32)
            parts = []
            for r in range(BLK):
                delta = delta_v[slot, r].astype(jnp.float32)
                parts.append(anchor[:, :HD] + key_scale * delta[:, :HD])
                parts.append(anchor[:, HD:] + value_scale * delta[:, HD:])
            tiles.append(jnp.concatenate(parts, axis=0))
        mixed = split(tiles)
        for t in range(NX):
            for c in range(CAP):
                send[k, t, c] = mixed[t * 16 : (t + 1) * 16, c * HD : (c + 1) * HD]
        mine = (y * NC + core) * PER_STEP + z * NX + x
        for d in range(NX):
            to = (x + d) & (NX - 1)
            copy = pltpu.make_async_remote_copy(
                send.at[k, to], arr.at[mine], send_sem.at[j], recv_sem.at[box],
                device_id=(session, to), device_id_type=MESH,
            )
            if d:
                copy.start()
            else:
                pl.when(k != SELF)(copy.start)

        @pl.when(k == SELF)
        def _():
            arr[mine] = send[SELF, x]

        return 0

    lax.fori_loop(0, NZ, send_session, 0)
    for d in range(1, NX):
        for copy in turn_copies(d):
            copy.start()
    qarr[x] = qsend[x]
    kvarr[x] = kvsend[x]
    lax.fori_loop(NZ, PLANES * NZ, send_session, 0)

    recv_rows = [recv_ref[c] for c in range(CAP)]
    dead = [jnp.where(row >= 0, 0.0, 1.0) for row in recv_rows]
    dead = jnp.concatenate(dead + [jnp.zeros((8 - CAP, PER_STEP * PLANES), jnp.float32)], axis=0)
    dead = dead.astype(jnp.bfloat16)
    holder = lax.broadcasted_iota(jnp.int32, (PER_STEP * PLANES, HD), 0)
    lane = lax.broadcasted_iota(jnp.int32, (PER_STEP * PLANES, HD), 1)
    line = jnp.zeros_like(lane)
    for i, dz in enumerate(Z_ORDER):
        line = jnp.where((lane >> 4) == i, ((z - dz) & (NZ - 1)) * PER_STEP, line)
    line = line + ((lane >> 2) & 3)

    def origin(j):
        dy, dc = offsets(j)
        return ((y - dy) & (NY - 1)) * NC + ((core - dc) & (NC - 1))

    def mark(j, _):
        pick = jnp.where(holder == line + origin(j) * NX, 1.0, 0.0).astype(jnp.bfloat16)
        bias_v[j] = jnp.dot(dead, pick, preferred_element_type=jnp.float32) * LOW
        return 0

    lax.fori_loop(0, PLANES, mark, 0)

    columns = jnp.concatenate(
        recv_rows + [jnp.full((8 - CAP, PER_STEP * PLANES), -1, jnp.int32)], axis=0
    ).T
    holder = lax.broadcasted_iota(jnp.int32, (PER_STEP * PLANES, 1), 0)
    place_of = (((holder >> 2) & 7) * PER_STEP + (holder >> 5) * NX + (holder & 3)) * 8
    for part in range(NBLK // HD):
        block = lax.broadcasted_iota(jnp.int32, (PER_STEP * PLANES, HD), 1) + part * HD
        found = jnp.zeros((PER_STEP * PLANES, HD), jnp.int32)
        for c in range(CAP):
            found = jnp.maximum(found, jnp.where(columns[:, c : c + 1] == block, place_of + c, 0))
        inv_v[part : part + 1, :] = jnp.max(found, axis=0, keepdims=True)
    inv_copy = pltpu.make_async_copy(inv_v, inv_ref, inv_sem)
    inv_copy.start()

    for d in range(1, NX):
        for copy in turn_copies(d):
            copy.wait()

    ones = jnp.ones((KEYS, HD), jnp.bfloat16)
    values[0, :, HD:] = ones
    values[1, :, HD:] = ones

    def unpack(count):
        for h in range(HEADS):
            keys[h, pl.ds(0, count), :] = flat[pl.ds(h, count, stride=4), :].astype(jnp.bfloat16)
            values[h, pl.ds(0, count), :HD] = flat[pl.ds(2 + h, count, stride=4), :].astype(
                jnp.bfloat16
            )

    flat[: TURN * 4, :] = kvarr[...].reshape(TURN * 4, HD).astype(jnp.float32)
    unpack(TURN)
    token = lax.broadcasted_iota(jnp.int32, (ROWS, TURN), 0) & (TOK - 1)
    position = lax.broadcasted_iota(jnp.int32, (ROWS, TURN), 1)
    for h in range(HEADS):
        for g in range(NX):
            scores = lax.dot_general(
                qarr[g, h], keys[h, :TURN, :], (((1,), (1,)), ((), ())),
                preferred_element_type=jnp.float32,
            )
            scores = jnp.where(position <= token + g * TOK, scores * SCALE2, LOW)
            peak = jnp.max(scores, axis=1, keepdims=True)
            power = jnp.exp2(scores - peak).astype(jnp.bfloat16)
            acc[h, g] = jnp.dot(power, values[h, :TURN, :], preferred_element_type=jnp.float32)
            top[h, g] = jnp.broadcast_to(peak, (ROWS, HD))

    def receive(j, box, count, z_from, z_to):
        first = origin(j) * PER_STEP
        span = arr.at[pl.ds(0, count)]
        pltpu.make_async_remote_copy(
            span, span, send_sem.at[0], recv_sem.at[box],
            device_id=(store, (x + 1) & (NX - 1)), device_id_type=MESH,
        ).wait_recv()
        lines = (z_to - z_from) * NX
        for i in range(z_from, z_to):
            at = first + ((z - Z_ORDER[i]) & (NZ - 1)) * NX
            for c in range(CAP):
                tiles = arr[pl.ds(at, NX), c].reshape(NX * 16, HD).astype(jnp.float32)
                flat[pl.ds((c * lines + (i - z_from) * NX) * 16, NX * 16), :] = tiles
        unpack(lines * CAP * BLK)
        rows = bias_v[j]
        return jnp.concatenate(
            [rows[c : c + 1, z_from * 16 : z_to * 16] for c in range(CAP)], axis=1
        )

    def update(bias, h, g):
        scores = lax.dot_general(
            qarr[g, h], keys[h, : bias.shape[1]], (((1,), (1,)), ((), ())),
            preferred_element_type=jnp.float32,
        )
        scores = scores * SCALE2 + bias
        before = top[h, g][:, 0:1]
        peak = jnp.maximum(before, jnp.max(scores, axis=1, keepdims=True))
        power = jnp.exp2(scores - peak).astype(jnp.bfloat16)
        total = acc[h, g] * jnp.exp2(before - peak) + jnp.dot(
            power, values[h, : bias.shape[1]], preferred_element_type=jnp.float32
        )
        return total, peak

    def attend(bias):
        for h in range(HEADS):
            for g in range(NX):
                acc[h, g], peak = update(bias, h, g)
                top[h, g] = jnp.broadcast_to(peak, (ROWS, HD))

    def step(j, _):
        attend(receive(j, j, PER_STEP, 0, NZ))
        return 0

    lax.fori_loop(0, PLANES - 1, step, 0)
    last, half = PLANES - 1, NZ // 2
    attend(receive(last, last, PER_STEP // 2 - 1, 0, half))
    bias = receive(last, last + 1, PER_STEP // 2, half, NZ)
    def back_copy(d):
        to = lax.rem(x + d, NX)
        return pltpu.make_async_remote_copy(
            outsend.at[to], outarr.at[x], back_send.at[d - 1], back_recv.at[d - 1],
            device_id=(store, to), device_id_type=MESH,
        )

    for d in (2, 1, 3, 0):
        g = lax.rem(x + d, NX)
        for h in range(HEADS):
            total, _ = update(bias, h, g)
            outsend[g, h] = (total[:, :HD] / total[:, HD:]).astype(jnp.bfloat16)
        if d:
            back_copy(d).start()
        else:
            outarr[x] = outsend[x]

    inv_copy.wait()

    def place(b, _):
        found = inv_ref[b >> 7, b & (HD - 1)]
        source = jnp.clip(found >> 3, 0, PLANES * PER_STEP - 1)
        stage[b] = arr[source, jnp.minimum(found & 7, CAP - 1)]
        return 0

    many = (NBLK + TURN_TILES) // PIECES
    moves = [
        pltpu.make_async_copy(
            stage.at[pl.ds(p * many, many)], cache_out.at[pl.ds(p * many, many)], out_sem.at[p]
        )
        for p in range(PIECES)
    ]
    stage[NBLK:] = kvarr[...].reshape(TURN_TILES, 16, HD)
    for p in range(PIECES):
        end = min((p + 1) * many, NBLK)
        lax.fori_loop(p * many, end, place, 0, unroll=8)
        moves[p].start()

    for d in range(1, NX):
        back_copy(d).wait()
    for t in range(NX):
        for hh in range(HEADS):
            for q in range(QPG):
                qf[q, pl.ds(t * 2 + hh, TOK, stride=8), :] = outarr[
                    t, hh, q * TOK : (q + 1) * TOK, :
                ].astype(jnp.float32)
    for q in range(QPG):
        att_v[:, :, q * HD : (q + 1) * HD] = qf[q].reshape(TOK, 8, HD).astype(jnp.bfloat16)

    for move in moves:
        move.wait()
    for j in range(PLANES):
        count = PER_STEP - 1 if j == last else PER_STEP
        span = arr.at[pl.ds(0, count)]
        pltpu.make_async_remote_copy(
            span, span, send_sem.at[j], recv_sem.at[j],
            device_id=(store, (x + 1) & (NX - 1)), device_id_type=MESH,
        ).wait_send()


def write_out(cache_in, att_in, cache_hbm, att_hbm, sems):
    copies = (
        pltpu.make_async_copy(cache_in, cache_hbm, sems.at[0]),
        pltpu.make_async_copy(att_in, att_hbm, sems.at[1]),
    )
    for copy in copies:
        copy.start()
    for copy in copies:
        copy.wait()


def shards(slot_anchor, slot_delta, slot_scale, send_slot, recv_block, turn_queries, turn_kv):
    bf16, f32 = jnp.bfloat16, jnp.float32
    slots = slot_anchor.shape[0]
    scales = slot_scale.transpose(1, 2, 0)
    cache_shape = (NBLK + TURN_TILES, 16, HD)
    in_hbm = pl.BlockSpec(memory_space=pltpu.HBM)
    in_vmem = pl.BlockSpec(memory_space=pltpu.VMEM)
    cache, attended = pl.pallas_call(
        body,
        out_shape=(
            pltpu.VMEM(cache_shape, bf16),
            pltpu.VMEM(turn_queries.shape, bf16),
        ),
        in_specs=[
            in_hbm, in_hbm, in_hbm, in_hbm, in_hbm, in_hbm, in_hbm,
        ],
        out_specs=(pl.BlockSpec(memory_space=pltpu.VMEM), pl.BlockSpec(memory_space=pltpu.VMEM)),
        scratch_shapes=[
            pltpu.VMEM(slot_anchor.shape, bf16),
            pltpu.VMEM(slot_delta.shape, bf16),
            pltpu.VMEM(scales.shape, bf16),
            pltpu.SMEM((CAP, 1, PLANES * NZ), jnp.int32),
            pltpu.VMEM((CAP, 1, PLANES * PER_STEP), jnp.int32),
            pltpu.VMEM(turn_queries.shape, bf16),
            pltpu.VMEM(turn_kv.shape, bf16),
            pltpu.VMEM(cache_shape, bf16),
            pltpu.VMEM((2, slots, 8, HD), f32),
            pltpu.VMEM((PLANES, 8, HD), f32),
            pltpu.VMEM((8, HD), jnp.int32),
            pltpu.SMEM((8, HD), jnp.int32),
            pltpu.VMEM((64, 64), bf16),
            pltpu.VMEM((QPG, TOK * 8, HD), f32),
            pltpu.VMEM((NX, HEADS, ROWS, HD), bf16),
            pltpu.VMEM((NX, HEADS, ROWS, HD), bf16),
            pltpu.VMEM((NX, TOK // BLK, 16, HD), bf16),
            pltpu.VMEM((NX, TOK // BLK, 16, HD), bf16),
            pltpu.VMEM((PLANES * NZ, NX, CAP, 16, HD), bf16),
            pltpu.VMEM((PLANES * PER_STEP, CAP, 16, HD), bf16),
            pltpu.VMEM((KEYS * 4, HD), f32),
            pltpu.VMEM((HEADS, KEYS, HD), bf16),
            pltpu.VMEM((HEADS, KEYS, 2 * HD), bf16),
            pltpu.VMEM((HEADS, NX, ROWS, 2 * HD), f32),
            pltpu.VMEM((HEADS, NX, ROWS, HD), f32),
            pltpu.VMEM((NX, HEADS, ROWS, HD), bf16),
            pltpu.VMEM((NX, HEADS, ROWS, HD), bf16),
            pltpu.SemaphoreType.DMA((7,)),
            pltpu.SemaphoreType.DMA((PLANES,)),
            pltpu.SemaphoreType.DMA((PLANES + 1,)),
            pltpu.SemaphoreType.DMA((2, NX - 1)),
            pltpu.SemaphoreType.DMA((2, NX - 1)),
            pltpu.SemaphoreType.DMA((NX - 1,)),
            pltpu.SemaphoreType.DMA((NX - 1,)),
            pltpu.SemaphoreType.DMA,
            pltpu.SemaphoreType.DMA((PIECES,)),
        ],
        compiler_params=pltpu.CompilerParams(
            collective_id=0, has_side_effects=True, vmem_limit_bytes=VMEM
        ),
        name="restore_attend",
    )(
        slot_anchor, slot_delta, scales, send_slot.transpose(2, 0, 1),
        recv_block.transpose(2, 0, 1), turn_queries, turn_kv,
    )
    cache, attended = pl.pallas_call(
        write_out,
        out_shape=(
            jax.ShapeDtypeStruct(cache_shape, bf16),
            jax.ShapeDtypeStruct(turn_queries.shape, bf16),
        ),
        in_specs=[in_vmem, in_vmem],
        out_specs=(in_hbm, in_hbm),
        scratch_shapes=[pltpu.SemaphoreType.DMA((2,))],
        compiler_params=pltpu.CompilerParams(vmem_limit_bytes=2**20),
        name="write_out",
    )(cache, attended)
    cache = cache.reshape(NBLK + TURN_TILES, BLK, 2, HEADS, HD).transpose(0, 1, 3, 2, 4)
    return cache.reshape(1, (NBLK + TURN_TILES) * BLK, HEADS, 2 * HD), attended


def solution(mesh):
    placed = (
        P(("store", "tp"), None, None),
        P(("store", "tp"), None, None, None),
        P(("store", "tp"), None, None),
        P(("store", "tp"), None, None),
        P("store", None, None),
        P(("store", "tp"), None, None),
        P(("store", "tp"), None, None),
    )
    return jax.shard_map(
        shards,
        mesh=mesh,
        in_specs=placed,
        out_specs=(P("store", None, "tp", None), P(("store", "tp"), None, None)),
        check_vma=False,
    )
```

```python
import math

import jax
import jax.numpy as jnp
from jax import lax
from jax.experimental import pallas as pl
from jax.experimental.pallas import tpu as pltpu
from jax.sharding import PartitionSpec as P

MESH = pl.DeviceIdType.MESH
NZ, NY, NC, NX = 8, 4, 2, 4
PLANES = NY * NC
PER_STEP = NZ * NX
CAP = 5
BLK = 4
HD = 128
QPG = 8
NBLK = 1024
TOK = 32
TURN = TOK * NX
HEADS = 2
ROWS = QPG * TOK
KEYS = PER_STEP * CAP * BLK
TURN_TILES = TURN // BLK
SCALE2 = math.log2(math.e) / math.sqrt(HD)
LOW = -1e30
Y_STEPS = sum(d << (2 * i) for i, d in enumerate((0, 0, 2, 2, 1, 3, 1, 3)))
C_STEPS = sum(d << i for i, d in enumerate((0, 1, 0, 1, 0, 1, 1, 0)))
Z_ORDER = (4, 3, 5, 0, 2, 6, 1, 7)
Z_STEPS = sum(d << (3 * i) for i, d in enumerate(Z_ORDER))
SELF = Z_ORDER.index(0)
PIECES = 8
VMEM = 62148608


def body(
    anchor_hbm, delta_hbm, scale_hbm, slot_hbm, recv_hbm, q_hbm, kv_hbm,
    cache_out, att_v,
    anchor_v, delta_v, scale_v, slot_ref, recv_ref, q_v, kv_v, stage, spread, bias_v, inv_v, inv_ref,
    perm, qf, qsend, qarr, kvsend, kvarr, send, arr,
    flat, keys, values, acc, top, outsend, outarr,
    load_sem, send_sem, recv_sem, turn_send, turn_recv, back_send, back_recv, inv_sem, out_sem, gate,
):
    store = lax.axis_index("store")
    x = lax.axis_index("tp")
    z, y, core = store // (NY * NC), (store // NC) % NY, store % NC

    loads = [
        pltpu.make_async_copy(src, dst, load_sem.at[i])
        for i, (src, dst) in enumerate(
            (
                (scale_hbm, scale_v), (slot_hbm, slot_ref), (anchor_hbm, anchor_v),
                (delta_hbm, delta_v), (q_hbm, q_v), (kv_hbm, kv_v), (recv_hbm, recv_ref),
            )
        )
    ]
    for load in loads:
        load.start()

    barrier = pltpu.get_barrier_semaphore()

    def on_line(n):
        z2, core2 = (z + (n >> 1)) & (NZ - 1), (core + (n & 1)) & (NC - 1)
        return ((z2 * NY + y) * NC + core2, x)

    def in_group(n):
        y2, x2 = (y + (n >> 2)) & (NY - 1), (x + (n & 3)) & (NX - 1)
        return ((z * NY + y2) * NC + core, x2)

    for n in range(1, 16):
        pl.semaphore_signal(barrier, inc=1, device_id=on_line(n), device_id_type=MESH)
        pl.semaphore_signal(barrier, inc=1, device_id=in_group(n), device_id_type=MESH)

    out_row = lax.broadcasted_iota(jnp.int32, (64, 64), 0)
    in_row = lax.broadcasted_iota(jnp.int32, (64, 64), 1)
    wanted = ((out_row >> 1) & 7) * 8 + (out_row >> 4) * 2 + (out_row & 1)
    perm[...] = jnp.where(in_row == wanted, 1.0, 0.0).astype(jnp.bfloat16)

    def split(tiles):
        wide = jnp.concatenate(tiles, axis=1).astype(jnp.bfloat16)
        return jnp.dot(perm[...], wide, preferred_element_type=jnp.float32).astype(jnp.bfloat16)

    loads[0].wait()
    scale = scale_v[...].astype(jnp.float32)
    slots = scale.shape[2]
    for kv in range(2):
        flat[kv * 8 : kv * 8 + 8, :] = scale[:, kv, :HD]
        flat[16 + kv * 8 : 24 + kv * 8, :] = scale[:, kv, HD : 2 * HD]
        flat[32 + kv * 8 : 40 + kv * 8, : slots - 2 * HD] = scale[:, kv, 2 * HD :]
    for slot in range(slots):
        part, lane = slot // HD * 16, slot % HD
        for kv in range(2):
            column = flat[part + kv * 8 : part + kv * 8 + 8, lane : lane + 1]
            spread[kv, slot] = jnp.broadcast_to(column, (8, HD))

    pl.semaphore_wait(barrier, 30)
    for n in range(1, 16):
        pl.semaphore_signal(gate, inc=1, device_id=in_group(n), device_id_type=MESH)

    def turn_copies(d):
        to = lax.rem(x + d, NX)
        return (
            pltpu.make_async_remote_copy(
                qsend.at[to], qarr.at[x], turn_send.at[0, d - 1], turn_recv.at[0, d - 1],
                device_id=(store, to), device_id_type=MESH,
            ),
            pltpu.make_async_remote_copy(
                kvsend.at[to], kvarr.at[x], turn_send.at[1, d - 1], turn_recv.at[1, d - 1],
                device_id=(store, to), device_id_type=MESH,
            ),
        )

    for load in loads[1:4]:
        load.wait()

    def offsets(j):
        return (Y_STEPS >> (2 * j)) & (NY - 1), (C_STEPS >> j) & (NC - 1)

    def z_offset(i):
        return (Z_STEPS >> (3 * i)) & (NZ - 1)

    def target(k):
        j, i = k >> 3, k & 7
        dy, dc = offsets(j)
        z2, y2, core2 = (z + z_offset(i)) & (NZ - 1), (y + dy) & (NY - 1), (core + dc) & (NC - 1)
        return (z2 * NY + y2) * NC + core2

    mine = (y * NC + core) * PER_STEP + z * NX + x

    def block_copy(k, d):
        to = (x + d) & (NX - 1)
        box = (k >> 3) + jnp.where(k >= (PLANES - 1) * NZ + NZ // 2, 1, 0)
        return pltpu.make_async_remote_copy(
            send.at[k, to], arr.at[mine], send_sem.at[k >> 3], recv_sem.at[box],
            device_id=(target(k), to), device_id_type=MESH,
        )

    def decode(k):
        session = target(k)
        tiles = []
        for c in range(CAP):
            slot = jnp.maximum(slot_ref[c, 0, session], 0)
            key_scale, value_scale = spread[0, slot], spread[1, slot]
            anchor = anchor_v[slot].astype(jnp.float32)
            parts = []
            for r in range(BLK):
                delta = delta_v[slot, r].astype(jnp.float32)
                parts.append(anchor[:, :HD] + key_scale * delta[:, :HD])
                parts.append(anchor[:, HD:] + value_scale * delta[:, HD:])
            tiles.append(jnp.concatenate(parts, axis=0))
        mixed = split(tiles)
        for t in range(NX):
            for c in range(CAP):
                send[k, t, c] = mixed[t * 16 : (t + 1) * 16, c * HD : (c + 1) * HD]

    def send_line(k, _):
        decode(k)
        pl.when(k != SELF)(block_copy(k, 0).start)
        return 0

    def send_rest(k, _):
        for d in range(1, NX):
            block_copy(k, d).start()
        return 0

    def send_all(k, _):
        decode(k)
        for d in range(NX):
            block_copy(k, d).start()
        return 0

    lax.fori_loop(0, 2 * NZ, send_line, 0)
    arr[mine] = send[SELF, x]
    pl.semaphore_wait(gate, 15)
    lax.fori_loop(0, 2 * NZ, send_rest, 0)
    loads[4].wait()
    for q in range(QPG):
        lanes = q_v[:, :, q * HD : (q + 1) * HD].astype(jnp.float32)
        qf[q] = lanes.reshape(TOK * 8, HD)
        for h in range(8):
            rows = qf[q, pl.ds(h, TOK, stride=8), :]
            qsend[h // 2, h % 2, q * TOK : (q + 1) * TOK, :] = rows.astype(jnp.bfloat16)
    loads[5].wait()
    turn_blocks = []
    for b in range(TOK // BLK):
        parts = []
        for r in range(BLK):
            row = kv_v[b * BLK + r].astype(jnp.float32)
            parts += [row[:, :HD], row[:, HD:]]
        turn_blocks.append(jnp.concatenate(parts, axis=0))
    mixed = split(turn_blocks)
    for t in range(NX):
        for b in range(TOK // BLK):
            kvsend[t, b] = mixed[t * 16 : (t + 1) * 16, b * HD : (b + 1) * HD]
    for d in range(1, NX):
        for copy in turn_copies(d):
            copy.start()
    qarr[x] = qsend[x]
    kvarr[x] = kvsend[x]
    lax.fori_loop(2 * NZ, PLANES * NZ, send_all, 0)
    loads[6].wait()

    recv_rows = [recv_ref[c] for c in range(CAP)]
    dead = [jnp.where(row >= 0, 0.0, 1.0) for row in recv_rows]
    dead = jnp.concatenate(dead + [jnp.zeros((8 - CAP, PER_STEP * PLANES), jnp.float32)], axis=0)
    dead = dead.astype(jnp.bfloat16)
    holder = lax.broadcasted_iota(jnp.int32, (PER_STEP * PLANES, HD), 0)
    lane = lax.broadcasted_iota(jnp.int32, (PER_STEP * PLANES, HD), 1)
    line = jnp.zeros_like(lane)
    for i, dz in enumerate(Z_ORDER):
        line = jnp.where((lane >> 4) == i, ((z - dz) & (NZ - 1)) * PER_STEP, line)
    line = line + ((lane >> 2) & 3)

    def origin(j):
        dy, dc = offsets(j)
        return ((y - dy) & (NY - 1)) * NC + ((core - dc) & (NC - 1))

    def mark(j, _):
        pick = jnp.where(holder == line + origin(j) * NX, 1.0, 0.0).astype(jnp.bfloat16)
        bias_v[j] = jnp.dot(dead, pick, preferred_element_type=jnp.float32) * LOW
        return 0

    lax.fori_loop(0, PLANES, mark, 0)

    columns = jnp.concatenate(
        recv_rows + [jnp.full((8 - CAP, PER_STEP * PLANES), -1, jnp.int32)], axis=0
    ).T
    holder = lax.broadcasted_iota(jnp.int32, (PER_STEP * PLANES, 1), 0)
    place_of = (((holder >> 2) & 7) * PER_STEP + (holder >> 5) * NX + (holder & 3)) * 8
    for part in range(NBLK // HD):
        block = lax.broadcasted_iota(jnp.int32, (PER_STEP * PLANES, HD), 1) + part * HD
        found = jnp.zeros((PER_STEP * PLANES, HD), jnp.int32)
        for c in range(CAP):
            found = jnp.maximum(found, jnp.where(columns[:, c : c + 1] == block, place_of + c, 0))
        inv_v[part : part + 1, :] = jnp.max(found, axis=0, keepdims=True)
    inv_copy = pltpu.make_async_copy(inv_v, inv_ref, inv_sem)
    inv_copy.start()

    for d in range(1, NX):
        for copy in turn_copies(d):
            copy.wait()

    ones = jnp.ones((KEYS, HD), jnp.bfloat16)
    values[0, :, HD:] = ones
    values[1, :, HD:] = ones

    def unpack(count):
        for h in range(HEADS):
            keys[h, pl.ds(0, count), :] = flat[pl.ds(h, count, stride=4), :].astype(jnp.bfloat16)
            values[h, pl.ds(0, count), :HD] = flat[pl.ds(2 + h, count, stride=4), :].astype(
                jnp.bfloat16
            )

    flat[: TURN * 4, :] = kvarr[...].reshape(TURN * 4, HD).astype(jnp.float32)
    unpack(TURN)
    token = lax.broadcasted_iota(jnp.int32, (ROWS, TURN), 0) & (TOK - 1)
    position = lax.broadcasted_iota(jnp.int32, (ROWS, TURN), 1)
    for h in range(HEADS):
        for g in range(NX):
            scores = lax.dot_general(
                qarr[g, h], keys[h, :TURN, :], (((1,), (1,)), ((), ())),
                preferred_element_type=jnp.float32,
            )
            scores = jnp.where(position <= token + g * TOK, scores * SCALE2, LOW)
            peak = jnp.max(scores, axis=1, keepdims=True)
            power = jnp.exp2(scores - peak).astype(jnp.bfloat16)
            acc[h, g] = jnp.dot(power, values[h, :TURN, :], preferred_element_type=jnp.float32)
            top[h, g] = jnp.broadcast_to(peak, (ROWS, HD))

    def receive(j, box, count, z_from, z_to):
        first = origin(j) * PER_STEP
        span = arr.at[pl.ds(0, count)]
        pltpu.make_async_remote_copy(
            span, span, send_sem.at[0], recv_sem.at[box],
            device_id=(store, (x + 1) & (NX - 1)), device_id_type=MESH,
        ).wait_recv()
        lines = (z_to - z_from) * NX
        for i in range(z_from, z_to):
            at = first + ((z - Z_ORDER[i]) & (NZ - 1)) * NX
            for c in range(CAP):
                tiles = arr[pl.ds(at, NX), c].reshape(NX * 16, HD).astype(jnp.float32)
                flat[pl.ds((c * lines + (i - z_from) * NX) * 16, NX * 16), :] = tiles
        unpack(lines * CAP * BLK)
        rows = bias_v[j]
        return jnp.concatenate(
            [rows[c : c + 1, z_from * 16 : z_to * 16] for c in range(CAP)], axis=1
        )

    def update(bias, h, g):
        scores = lax.dot_general(
            qarr[g, h], keys[h, : bias.shape[1]], (((1,), (1,)), ((), ())),
            preferred_element_type=jnp.float32,
        )
        scores = scores * SCALE2 + bias
        before = top[h, g][:, 0:1]
        peak = jnp.maximum(before, jnp.max(scores, axis=1, keepdims=True))
        power = jnp.exp2(scores - peak).astype(jnp.bfloat16)
        total = acc[h, g] * jnp.exp2(before - peak) + jnp.dot(
            power, values[h, : bias.shape[1]], preferred_element_type=jnp.float32
        )
        return total, peak

    def attend(bias):
        for h in range(HEADS):
            for g in range(NX):
                acc[h, g], peak = update(bias, h, g)
                top[h, g] = jnp.broadcast_to(peak, (ROWS, HD))

    def step(j, _):
        attend(receive(j, j, PER_STEP, 0, NZ))
        return 0

    attend(receive(0, 0, PER_STEP - 1, 0, NZ))
    lax.fori_loop(1, PLANES - 1, step, 0)
    last, half = PLANES - 1, NZ // 2
    attend(receive(last, last, PER_STEP // 2, 0, half))
    bias = receive(last, last + 1, PER_STEP // 2, half, NZ)
    def back_copy(d, h):
        to = (x + d) & (NX - 1)
        return pltpu.make_async_remote_copy(
            outsend.at[to, h], outarr.at[x, h], back_send.at[d - 1, h], back_recv.at[d - 1, h],
            device_id=(store, to), device_id_type=MESH,
        )

    for d in (2, 1, 3, 0):
        g = (x + d) & (NX - 1)
        for h in range(HEADS):
            total, _ = update(bias, h, g)
            outsend[g, h] = (total[:, :HD] / total[:, HD:]).astype(jnp.bfloat16)
            if d:
                back_copy(d, h).start()
    outarr[x] = outsend[x]

    inv_copy.wait()

    def place(b, _):
        found = inv_ref[b >> 7, b & (HD - 1)]
        source = jnp.clip(found >> 3, 0, PLANES * PER_STEP - 1)
        stage[b] = arr[source, jnp.minimum(found & 7, CAP - 1)]
        return 0

    many = (NBLK + TURN_TILES) // PIECES
    moves = [
        pltpu.make_async_copy(
            stage.at[pl.ds(p * many, many)], cache_out.at[pl.ds(p * many, many)], out_sem.at[p]
        )
        for p in range(PIECES)
    ]
    stage[NBLK:] = kvarr[...].reshape(TURN_TILES, 16, HD)
    for p in range(PIECES):
        end = min((p + 1) * many, NBLK)
        lax.fori_loop(p * many, end, place, 0, unroll=8)
        moves[p].start()

    for d in range(1, NX):
        for h in range(HEADS):
            back_copy(d, h).wait()
    for t in range(NX):
        for hh in range(HEADS):
            for q in range(QPG):
                qf[q, pl.ds(t * 2 + hh, TOK, stride=8), :] = outarr[
                    t, hh, q * TOK : (q + 1) * TOK, :
                ].astype(jnp.float32)
    for q in range(QPG):
        att_v[:, :, q * HD : (q + 1) * HD] = qf[q].reshape(TOK, 8, HD).astype(jnp.bfloat16)

    for move in moves:
        move.wait()
    for j in range(PLANES):
        count = PER_STEP - 1 if j == 0 else PER_STEP
        span = arr.at[pl.ds(0, count)]
        pltpu.make_async_remote_copy(
            span, span, send_sem.at[j], recv_sem.at[j],
            device_id=(store, (x + 1) & (NX - 1)), device_id_type=MESH,
        ).wait_send()


def write_out(cache_in, att_in, cache_hbm, att_hbm, sems):
    copies = (
        pltpu.make_async_copy(cache_in, cache_hbm, sems.at[0]),
        pltpu.make_async_copy(att_in, att_hbm, sems.at[1]),
    )
    for copy in copies:
        copy.start()
    for copy in copies:
        copy.wait()


def shards(slot_anchor, slot_delta, slot_scale, send_slot, recv_block, turn_queries, turn_kv):
    bf16, f32 = jnp.bfloat16, jnp.float32
    slots = slot_anchor.shape[0]
    scales = slot_scale.transpose(1, 2, 0)
    cache_shape = (NBLK + TURN_TILES, 16, HD)
    in_hbm = pl.BlockSpec(memory_space=pltpu.HBM)
    in_vmem = pl.BlockSpec(memory_space=pltpu.VMEM)
    cache, attended = pl.pallas_call(
        body,
        out_shape=(
            pltpu.VMEM(cache_shape, bf16),
            pltpu.VMEM(turn_queries.shape, bf16),
        ),
        in_specs=[
            in_hbm, in_hbm, in_hbm, in_hbm, in_hbm, in_hbm, in_hbm,
        ],
        out_specs=(pl.BlockSpec(memory_space=pltpu.VMEM), pl.BlockSpec(memory_space=pltpu.VMEM)),
        scratch_shapes=[
            pltpu.VMEM(slot_anchor.shape, bf16),
            pltpu.VMEM(slot_delta.shape, bf16),
            pltpu.VMEM(scales.shape, bf16),
            pltpu.SMEM((CAP, 1, PLANES * NZ), jnp.int32),
            pltpu.VMEM((CAP, 1, PLANES * PER_STEP), jnp.int32),
            pltpu.VMEM(turn_queries.shape, bf16),
            pltpu.VMEM(turn_kv.shape, bf16),
            pltpu.VMEM(cache_shape, bf16),
            pltpu.VMEM((2, slots, 8, HD), f32),
            pltpu.VMEM((PLANES, 8, HD), f32),
            pltpu.VMEM((8, HD), jnp.int32),
            pltpu.SMEM((8, HD), jnp.int32),
            pltpu.VMEM((64, 64), bf16),
            pltpu.VMEM((QPG, TOK * 8, HD), f32),
            pltpu.VMEM((NX, HEADS, ROWS, HD), bf16),
            pltpu.VMEM((NX, HEADS, ROWS, HD), bf16),
            pltpu.VMEM((NX, TOK // BLK, 16, HD), bf16),
            pltpu.VMEM((NX, TOK // BLK, 16, HD), bf16),
            pltpu.VMEM((PLANES * NZ, NX, CAP, 16, HD), bf16),
            pltpu.VMEM((PLANES * PER_STEP, CAP, 16, HD), bf16),
            pltpu.VMEM((KEYS * 4, HD), f32),
            pltpu.VMEM((HEADS, KEYS, HD), bf16),
            pltpu.VMEM((HEADS, KEYS, 2 * HD), bf16),
            pltpu.VMEM((HEADS, NX, ROWS, 2 * HD), f32),
            pltpu.VMEM((HEADS, NX, ROWS, HD), f32),
            pltpu.VMEM((NX, HEADS, ROWS, HD), bf16),
            pltpu.VMEM((NX, HEADS, ROWS, HD), bf16),
            pltpu.SemaphoreType.DMA((7,)),
            pltpu.SemaphoreType.DMA((PLANES,)),
            pltpu.SemaphoreType.DMA((PLANES + 1,)),
            pltpu.SemaphoreType.DMA((2, NX - 1)),
            pltpu.SemaphoreType.DMA((2, NX - 1)),
            pltpu.SemaphoreType.DMA((NX - 1, HEADS)),
            pltpu.SemaphoreType.DMA((NX - 1, HEADS)),
            pltpu.SemaphoreType.DMA,
            pltpu.SemaphoreType.DMA((PIECES,)),
            pltpu.SemaphoreType.REGULAR,
        ],
        compiler_params=pltpu.CompilerParams(
            collective_id=0, has_side_effects=True, vmem_limit_bytes=VMEM
        ),
        name="restore_attend",
    )(
        slot_anchor, slot_delta, scales, send_slot.transpose(2, 0, 1),
        recv_block.transpose(2, 0, 1), turn_queries, turn_kv,
    )
    cache, attended = pl.pallas_call(
        write_out,
        out_shape=(
            jax.ShapeDtypeStruct(cache_shape, bf16),
            jax.ShapeDtypeStruct(turn_queries.shape, bf16),
        ),
        in_specs=[in_vmem, in_vmem],
        out_specs=(in_hbm, in_hbm),
        scratch_shapes=[pltpu.SemaphoreType.DMA((2,))],
        compiler_params=pltpu.CompilerParams(vmem_limit_bytes=2**20),
        name="write_out",
    )(cache, attended)
    cache = cache.reshape(NBLK + TURN_TILES, BLK, 2, HEADS, HD).transpose(0, 1, 3, 2, 4)
    return cache.reshape(1, (NBLK + TURN_TILES) * BLK, HEADS, 2 * HD), attended


def solution(mesh):
    placed = (
        P(("store", "tp"), None, None),
        P(("store", "tp"), None, None, None),
        P(("store", "tp"), None, None),
        P(("store", "tp"), None, None),
        P("store", None, None),
        P(("store", "tp"), None, None),
        P(("store", "tp"), None, None),
    )
    return jax.shard_map(
        shards,
        mesh=mesh,
        in_specs=placed,
        out_specs=(P("store", None, "tp", None), P(("store", "tp"), None, None)),
        check_vma=False,
    )
```

```python
import math

import jax
import jax.numpy as jnp
from jax import lax
from jax.experimental import pallas as pl
from jax.experimental.pallas import tpu as pltpu
from jax.sharding import PartitionSpec as P

MESH = pl.DeviceIdType.MESH
NZ, NY, NC, NX = 8, 4, 2, 4
PLANES = NY * NC
PER_STEP = NZ * NX
CAP = 5
BLK = 4
HD = 128
QPG = 8
NBLK = 1024
TOK = 32
TURN = TOK * NX
HEADS = 2
ROWS = QPG * TOK
KEYS = PER_STEP * CAP * BLK
TURN_TILES = TURN // BLK
SCALE2 = math.log2(math.e) / math.sqrt(HD)
LOW = -1e30
Y_STEPS = sum(d << (2 * i) for i, d in enumerate((0, 0, 2, 2, 1, 3, 1, 3)))
C_STEPS = sum(d << i for i, d in enumerate((0, 1, 0, 1, 0, 1, 1, 0)))
Z_ORDER = (4, 3, 5, 0, 2, 6, 1, 7)
Z_STEPS = sum(d << (3 * i) for i, d in enumerate(Z_ORDER))
SELF = Z_ORDER.index(0)
PIECES = 8
VMEM = 62148608


def body(
    anchor_hbm, delta_hbm, scale_hbm, slot_hbm, recv_hbm, q_hbm, kv_hbm,
    cache_out, att_v,
    anchor_v, delta_v, scale_v, slot_ref, recv_ref, q_v, kv_v, stage, spread, bias_v, inv_v, inv_ref,
    perm, qf, qsend, qarr, kvsend, kvarr, send, arr,
    flat, keys, values, acc, top, outsend, outarr,
    load_sem, send_sem, recv_sem, turn_send, turn_recv, back_send, back_recv, inv_sem, out_sem, gate,
):
    store = lax.axis_index("store")
    x = lax.axis_index("tp")
    z, y, core = store // (NY * NC), (store // NC) % NY, store % NC

    loads = [
        pltpu.make_async_copy(src, dst, load_sem.at[i])
        for i, (src, dst) in enumerate(
            (
                (scale_hbm, scale_v), (slot_hbm, slot_ref), (anchor_hbm, anchor_v),
                (delta_hbm, delta_v), (q_hbm, q_v), (kv_hbm, kv_v), (recv_hbm, recv_ref),
            )
        )
    ]
    for load in loads:
        load.start()

    barrier = pltpu.get_barrier_semaphore()

    def on_line(n):
        z2, core2 = (z + (n >> 1)) & (NZ - 1), (core + (n & 1)) & (NC - 1)
        return ((z2 * NY + y) * NC + core2, x)

    def in_group(n):
        y2, x2 = (y + (n >> 2)) & (NY - 1), (x + (n & 3)) & (NX - 1)
        return ((z * NY + y2) * NC + core, x2)

    for n in range(1, 16):
        pl.semaphore_signal(barrier, inc=1, device_id=on_line(n), device_id_type=MESH)
        pl.semaphore_signal(barrier, inc=1, device_id=in_group(n), device_id_type=MESH)

    out_row = lax.broadcasted_iota(jnp.int32, (64, 64), 0)
    in_row = lax.broadcasted_iota(jnp.int32, (64, 64), 1)
    wanted = ((out_row >> 1) & 7) * 8 + (out_row >> 4) * 2 + (out_row & 1)
    perm[...] = jnp.where(in_row == wanted, 1.0, 0.0).astype(jnp.bfloat16)

    def split(tiles):
        wide = jnp.concatenate(tiles, axis=1).astype(jnp.bfloat16)
        return jnp.dot(perm[...], wide, preferred_element_type=jnp.float32).astype(jnp.bfloat16)

    loads[0].wait()
    scale = scale_v[...].astype(jnp.float32)
    slots = scale.shape[2]
    for kv in range(2):
        flat[kv * 8 : kv * 8 + 8, :] = scale[:, kv, :HD]
        flat[16 + kv * 8 : 24 + kv * 8, :] = scale[:, kv, HD : 2 * HD]
        flat[32 + kv * 8 : 40 + kv * 8, : slots - 2 * HD] = scale[:, kv, 2 * HD :]
    for slot in range(slots):
        part, lane = slot // HD * 16, slot % HD
        for kv in range(2):
            column = flat[part + kv * 8 : part + kv * 8 + 8, lane : lane + 1]
            spread[kv, slot] = jnp.broadcast_to(column, (8, HD))

    pl.semaphore_wait(barrier, 30)
    for n in range(1, 16):
        pl.semaphore_signal(gate, inc=1, device_id=in_group(n), device_id_type=MESH)

    def turn_copies(d):
        to = lax.rem(x + d, NX)
        return (
            pltpu.make_async_remote_copy(
                qsend.at[to], qarr.at[x], turn_send.at[0, d - 1], turn_recv.at[0, d - 1],
                device_id=(store, to), device_id_type=MESH,
            ),
            pltpu.make_async_remote_copy(
                kvsend.at[to], kvarr.at[x], turn_send.at[1, d - 1], turn_recv.at[1, d - 1],
                device_id=(store, to), device_id_type=MESH,
            ),
        )

    for load in loads[1:4]:
        load.wait()

    def offsets(j):
        return (Y_STEPS >> (2 * j)) & (NY - 1), (C_STEPS >> j) & (NC - 1)

    def z_offset(i):
        return (Z_STEPS >> (3 * i)) & (NZ - 1)

    def target(k):
        j, i = k >> 3, k & 7
        dy, dc = offsets(j)
        z2, y2, core2 = (z + z_offset(i)) & (NZ - 1), (y + dy) & (NY - 1), (core + dc) & (NC - 1)
        return (z2 * NY + y2) * NC + core2

    mine = (y * NC + core) * PER_STEP + z * NX + x

    def block_copy(k, d):
        to = (x + d) & (NX - 1)
        box = (k >> 3) + jnp.where(k >= (PLANES - 1) * NZ + NZ // 2, 1, 0)
        return pltpu.make_async_remote_copy(
            send.at[k, to], arr.at[pl.ds(mine * CAP, CAP)], send_sem.at[k >> 3], recv_sem.at[box],
            device_id=(target(k), to), device_id_type=MESH,
        )

    def decode(k):
        session = target(k)
        tiles = []
        for c in range(CAP):
            slot = jnp.maximum(slot_ref[c, 0, session], 0)
            key_scale, value_scale = spread[0, slot], spread[1, slot]
            anchor = anchor_v[slot].astype(jnp.float32)
            parts = []
            for r in range(BLK):
                delta = delta_v[slot, r].astype(jnp.float32)
                parts.append(anchor[:, :HD] + key_scale * delta[:, :HD])
                parts.append(anchor[:, HD:] + value_scale * delta[:, HD:])
            tiles.append(jnp.concatenate(parts, axis=0))
        mixed = split(tiles)
        for t in range(NX):
            for c in range(CAP):
                send[k, t, c] = mixed[t * 16 : (t + 1) * 16, c * HD : (c + 1) * HD]

    def send_line(k, _):
        decode(k)
        pl.when(k != SELF)(block_copy(k, 0).start)
        return 0

    def send_rest(k, _):
        for d in range(1, NX):
            block_copy(k, d).start()
        return 0

    def send_all(k, _):
        decode(k)
        for d in range(NX):
            block_copy(k, d).start()
        return 0

    lax.fori_loop(0, 2 * NZ, send_line, 0, unroll=4)
    arr[pl.ds(mine * CAP, CAP)] = send[SELF, x]
    pl.semaphore_wait(gate, 15)
    lax.fori_loop(0, 2 * NZ, send_rest, 0)
    loads[4].wait()
    for q in range(QPG):
        lanes = q_v[:, :, q * HD : (q + 1) * HD].astype(jnp.float32)
        qf[q] = lanes.reshape(TOK * 8, HD)
        for h in range(8):
            rows = qf[q, pl.ds(h, TOK, stride=8), :]
            qsend[h // 2, h % 2, q * TOK : (q + 1) * TOK, :] = rows.astype(jnp.bfloat16)
    loads[5].wait()
    turn_blocks = []
    for b in range(TOK // BLK):
        parts = []
        for r in range(BLK):
            row = kv_v[b * BLK + r].astype(jnp.float32)
            parts += [row[:, :HD], row[:, HD:]]
        turn_blocks.append(jnp.concatenate(parts, axis=0))
    mixed = split(turn_blocks)
    for t in range(NX):
        for b in range(TOK // BLK):
            kvsend[t, b] = mixed[t * 16 : (t + 1) * 16, b * HD : (b + 1) * HD]
    for d in range(1, NX):
        for copy in turn_copies(d):
            copy.start()
    qarr[x] = qsend[x]
    kvarr[x] = kvsend[x]
    lax.fori_loop(2 * NZ, PLANES * NZ, send_all, 0, unroll=4)
    loads[6].wait()

    recv_rows = [recv_ref[c] for c in range(CAP)]
    dead = [jnp.where(row >= 0, 0.0, 1.0) for row in recv_rows]
    dead = jnp.concatenate(dead + [jnp.zeros((8 - CAP, PER_STEP * PLANES), jnp.float32)], axis=0)
    dead = dead.astype(jnp.bfloat16)
    holder = lax.broadcasted_iota(jnp.int32, (PER_STEP * PLANES, HD), 0)
    lane = lax.broadcasted_iota(jnp.int32, (PER_STEP * PLANES, HD), 1)
    line = jnp.zeros_like(lane)
    for i, dz in enumerate(Z_ORDER):
        line = jnp.where((lane >> 4) == i, ((z - dz) & (NZ - 1)) * PER_STEP, line)
    line = line + ((lane >> 2) & 3)

    def origin(j):
        dy, dc = offsets(j)
        return ((y - dy) & (NY - 1)) * NC + ((core - dc) & (NC - 1))

    def mark(j, _):
        pick = jnp.where(holder == line + origin(j) * NX, 1.0, 0.0).astype(jnp.bfloat16)
        bias_v[j] = jnp.dot(dead, pick, preferred_element_type=jnp.float32) * LOW
        return 0

    lax.fori_loop(0, PLANES, mark, 0)

    columns = jnp.concatenate(
        recv_rows + [jnp.full((8 - CAP, PER_STEP * PLANES), -1, jnp.int32)], axis=0
    ).T
    holder = lax.broadcasted_iota(jnp.int32, (PER_STEP * PLANES, 1), 0)
    place_of = (((holder >> 2) & 7) * PER_STEP + (holder >> 5) * NX + (holder & 3)) * CAP
    for part in range(NBLK // HD):
        block = lax.broadcasted_iota(jnp.int32, (PER_STEP * PLANES, HD), 1) + part * HD
        found = jnp.zeros((PER_STEP * PLANES, HD), jnp.int32)
        for c in range(CAP):
            found = jnp.maximum(found, jnp.where(columns[:, c : c + 1] == block, place_of + c, 0))
        inv_v[part : part + 1, :] = jnp.max(found, axis=0, keepdims=True)
    inv_copy = pltpu.make_async_copy(inv_v, inv_ref, inv_sem)
    inv_copy.start()

    for d in range(1, NX):
        for copy in turn_copies(d):
            copy.wait()

    ones = jnp.ones((KEYS, HD), jnp.bfloat16)
    values[0, :, HD:] = ones
    values[1, :, HD:] = ones

    def unpack(count):
        for h in range(HEADS):
            keys[h, pl.ds(0, count), :] = flat[pl.ds(h, count, stride=4), :].astype(jnp.bfloat16)
            values[h, pl.ds(0, count), :HD] = flat[pl.ds(2 + h, count, stride=4), :].astype(
                jnp.bfloat16
            )

    flat[: TURN * 4, :] = kvarr[...].reshape(TURN * 4, HD).astype(jnp.float32)
    unpack(TURN)
    token = lax.broadcasted_iota(jnp.int32, (ROWS, TURN), 0) & (TOK - 1)
    position = lax.broadcasted_iota(jnp.int32, (ROWS, TURN), 1)
    for h in range(HEADS):
        for g in range(NX):
            scores = lax.dot_general(
                qarr[g, h], keys[h, :TURN, :], (((1,), (1,)), ((), ())),
                preferred_element_type=jnp.float32,
            )
            scores = jnp.where(position <= token + g * TOK, scores * SCALE2, LOW)
            peak = jnp.max(scores, axis=1, keepdims=True)
            power = jnp.exp2(scores - peak).astype(jnp.bfloat16)
            acc[h, g] = jnp.dot(power, values[h, :TURN, :], preferred_element_type=jnp.float32)
            top[h, g] = jnp.broadcast_to(peak, (ROWS, HD))

    def receive(j, box, count, z_from, z_to):
        first = origin(j) * (PER_STEP * CAP)
        span = arr.at[pl.ds(0, count * CAP)]
        pltpu.make_async_remote_copy(
            span, span, send_sem.at[0], recv_sem.at[box],
            device_id=(store, (x + 1) & (NX - 1)), device_id_type=MESH,
        ).wait_recv()
        lines = (z_to - z_from) * NX
        for i in range(z_from, z_to):
            at = first + ((z - Z_ORDER[i]) & (NZ - 1)) * (NX * CAP)
            for n in range(NX):
                for c in range(CAP):
                    row = (c * lines + (i - z_from) * NX + n) * 16
                    flat[row : row + 16, :] = arr[at + n * CAP + c].astype(jnp.float32)
        unpack(lines * CAP * BLK)
        rows = bias_v[j]
        return jnp.concatenate(
            [rows[c : c + 1, z_from * 16 : z_to * 16] for c in range(CAP)], axis=1
        )

    def update(bias, h, g):
        scores = lax.dot_general(
            qarr[g, h], keys[h, : bias.shape[1]], (((1,), (1,)), ((), ())),
            preferred_element_type=jnp.float32,
        )
        scores = scores * SCALE2 + bias
        before = top[h, g][:, 0:1]
        peak = jnp.maximum(before, jnp.max(scores, axis=1, keepdims=True))
        power = jnp.exp2(scores - peak).astype(jnp.bfloat16)
        total = acc[h, g] * jnp.exp2(before - peak) + jnp.dot(
            power, values[h, : bias.shape[1]], preferred_element_type=jnp.float32
        )
        return total, peak

    def attend(bias):
        for h in range(HEADS):
            for g in range(NX):
                acc[h, g], peak = update(bias, h, g)
                top[h, g] = jnp.broadcast_to(peak, (ROWS, HD))

    def step(j, _):
        attend(receive(j, j, PER_STEP, 0, NZ))
        return 0

    attend(receive(0, 0, PER_STEP - 1, 0, NZ))
    lax.fori_loop(1, PLANES - 1, step, 0)
    last, half = PLANES - 1, NZ // 2
    attend(receive(last, last, PER_STEP // 2, 0, half))
    bias = receive(last, last + 1, PER_STEP // 2, half, NZ)
    def back_copy(d, h):
        to = (x + d) & (NX - 1)
        return pltpu.make_async_remote_copy(
            outsend.at[to, h], outarr.at[x, h], back_send.at[d - 1, h], back_recv.at[d - 1, h],
            device_id=(store, to), device_id_type=MESH,
        )

    for d in (2, 1, 3, 0):
        g = (x + d) & (NX - 1)
        for h in range(HEADS):
            total, _ = update(bias, h, g)
            outsend[g, h] = (total[:, :HD] / total[:, HD:]).astype(jnp.bfloat16)
            if d:
                back_copy(d, h).start()
    outarr[x] = outsend[x]

    inv_copy.wait()

    def place(b, _):
        stage[b] = arr[inv_ref[b >> 7, b & (HD - 1)]]
        return 0

    many = (NBLK + TURN_TILES) // PIECES
    moves = [
        pltpu.make_async_copy(
            stage.at[pl.ds(p * many, many)], cache_out.at[pl.ds(p * many, many)], out_sem.at[p]
        )
        for p in range(PIECES)
    ]
    stage[NBLK:] = kvarr[...].reshape(TURN_TILES, 16, HD)
    for p in range(PIECES):
        end = min((p + 1) * many, NBLK)
        lax.fori_loop(p * many, end, place, 0, unroll=8)
        moves[p].start()

    for d in range(1, NX):
        for h in range(HEADS):
            back_copy(d, h).wait()
    for t in range(NX):
        for hh in range(HEADS):
            for q in range(QPG):
                qf[q, pl.ds(t * 2 + hh, TOK, stride=8), :] = outarr[
                    t, hh, q * TOK : (q + 1) * TOK, :
                ].astype(jnp.float32)
    for q in range(QPG):
        att_v[:, :, q * HD : (q + 1) * HD] = qf[q].reshape(TOK, 8, HD).astype(jnp.bfloat16)

    for move in moves:
        move.wait()
    for j in range(PLANES):
        count = PER_STEP - 1 if j == 0 else PER_STEP
        span = arr.at[pl.ds(0, count * CAP)]
        pltpu.make_async_remote_copy(
            span, span, send_sem.at[j], recv_sem.at[j],
            device_id=(store, (x + 1) & (NX - 1)), device_id_type=MESH,
        ).wait_send()


def write_out(cache_in, att_in, cache_hbm, att_hbm, sems):
    copies = (
        pltpu.make_async_copy(cache_in, cache_hbm, sems.at[0]),
        pltpu.make_async_copy(att_in, att_hbm, sems.at[1]),
    )
    for copy in copies:
        copy.start()
    for copy in copies:
        copy.wait()


def shards(slot_anchor, slot_delta, slot_scale, send_slot, recv_block, turn_queries, turn_kv):
    bf16, f32 = jnp.bfloat16, jnp.float32
    slots = slot_anchor.shape[0]
    scales = slot_scale.transpose(1, 2, 0)
    cache_shape = (NBLK + TURN_TILES, 16, HD)
    in_hbm = pl.BlockSpec(memory_space=pltpu.HBM)
    in_vmem = pl.BlockSpec(memory_space=pltpu.VMEM)
    cache, attended = pl.pallas_call(
        body,
        out_shape=(
            pltpu.VMEM(cache_shape, bf16),
            pltpu.VMEM(turn_queries.shape, bf16),
        ),
        in_specs=[
            in_hbm, in_hbm, in_hbm, in_hbm, in_hbm, in_hbm, in_hbm,
        ],
        out_specs=(pl.BlockSpec(memory_space=pltpu.VMEM), pl.BlockSpec(memory_space=pltpu.VMEM)),
        scratch_shapes=[
            pltpu.VMEM(slot_anchor.shape, bf16),
            pltpu.VMEM(slot_delta.shape, bf16),
            pltpu.VMEM(scales.shape, bf16),
            pltpu.SMEM((CAP, 1, PLANES * NZ), jnp.int32),
            pltpu.VMEM((CAP, 1, PLANES * PER_STEP), jnp.int32),
            pltpu.VMEM(turn_queries.shape, bf16),
            pltpu.VMEM(turn_kv.shape, bf16),
            pltpu.VMEM(cache_shape, bf16),
            pltpu.VMEM((2, slots, 8, HD), f32),
            pltpu.VMEM((PLANES, 8, HD), f32),
            pltpu.VMEM((8, HD), jnp.int32),
            pltpu.SMEM((8, HD), jnp.int32),
            pltpu.VMEM((64, 64), bf16),
            pltpu.VMEM((QPG, TOK * 8, HD), f32),
            pltpu.VMEM((NX, HEADS, ROWS, HD), bf16),
            pltpu.VMEM((NX, HEADS, ROWS, HD), bf16),
            pltpu.VMEM((NX, TOK // BLK, 16, HD), bf16),
            pltpu.VMEM((NX, TOK // BLK, 16, HD), bf16),
            pltpu.VMEM((PLANES * NZ, NX, CAP, 16, HD), bf16),
            pltpu.VMEM((PLANES * PER_STEP * CAP, 16, HD), bf16),
            pltpu.VMEM((KEYS * 4, HD), f32),
            pltpu.VMEM((HEADS, KEYS, HD), bf16),
            pltpu.VMEM((HEADS, KEYS, 2 * HD), bf16),
            pltpu.VMEM((HEADS, NX, ROWS, 2 * HD), f32),
            pltpu.VMEM((HEADS, NX, ROWS, HD), f32),
            pltpu.VMEM((NX, HEADS, ROWS, HD), bf16),
            pltpu.VMEM((NX, HEADS, ROWS, HD), bf16),
            pltpu.SemaphoreType.DMA((7,)),
            pltpu.SemaphoreType.DMA((PLANES,)),
            pltpu.SemaphoreType.DMA((PLANES + 1,)),
            pltpu.SemaphoreType.DMA((2, NX - 1)),
            pltpu.SemaphoreType.DMA((2, NX - 1)),
            pltpu.SemaphoreType.DMA((NX - 1, HEADS)),
            pltpu.SemaphoreType.DMA((NX - 1, HEADS)),
            pltpu.SemaphoreType.DMA,
            pltpu.SemaphoreType.DMA((PIECES,)),
            pltpu.SemaphoreType.REGULAR,
        ],
        compiler_params=pltpu.CompilerParams(
            collective_id=0, has_side_effects=True, vmem_limit_bytes=VMEM
        ),
        name="restore_attend",
    )(
        slot_anchor, slot_delta, scales, send_slot.transpose(2, 0, 1),
        recv_block.transpose(2, 0, 1), turn_queries, turn_kv,
    )
    cache, attended = pl.pallas_call(
        write_out,
        out_shape=(
            jax.ShapeDtypeStruct(cache_shape, bf16),
            jax.ShapeDtypeStruct(turn_queries.shape, bf16),
        ),
        in_specs=[in_vmem, in_vmem],
        out_specs=(in_hbm, in_hbm),
        scratch_shapes=[pltpu.SemaphoreType.DMA((2,))],
        compiler_params=pltpu.CompilerParams(vmem_limit_bytes=2**20),
        name="write_out",
    )(cache, attended)
    cache = cache.reshape(NBLK + TURN_TILES, BLK, 2, HEADS, HD).transpose(0, 1, 3, 2, 4)
    return cache.reshape(1, (NBLK + TURN_TILES) * BLK, HEADS, 2 * HD), attended


def solution(mesh):
    placed = (
        P(("store", "tp"), None, None),
        P(("store", "tp"), None, None, None),
        P(("store", "tp"), None, None),
        P(("store", "tp"), None, None),
        P("store", None, None),
        P(("store", "tp"), None, None),
        P(("store", "tp"), None, None),
    )
    return jax.shard_map(
        shards,
        mesh=mesh,
        in_specs=placed,
        out_specs=(P("store", None, "tp", None), P(("store", "tp"), None, None)),
        check_vma=False,
    )
```

```python
import math

import jax
import jax.numpy as jnp
from jax import lax
from jax.experimental import pallas as pl
from jax.experimental.pallas import tpu as pltpu
from jax.sharding import PartitionSpec as P

MESH = pl.DeviceIdType.MESH
NZ, NY, NC, NX = 8, 4, 2, 4
PLANES = NY * NC
PER_STEP = NZ * NX
CAP = 5
BLK = 4
HD = 128
QPG = 8
NBLK = 1024
TOK = 32
TURN = TOK * NX
HEADS = 2
ROWS = QPG * TOK
KEYS = PER_STEP * CAP * BLK
TURN_TILES = TURN // BLK
SCALE2 = math.log2(math.e) / math.sqrt(HD)
LOW = -1e30
Y_STEPS = sum(d << (2 * i) for i, d in enumerate((0, 0, 2, 2, 1, 3, 1, 3)))
C_STEPS = sum(d << i for i, d in enumerate((0, 1, 0, 1, 0, 1, 1, 0)))
Z_ORDER = (4, 3, 5, 0, 2, 6, 1, 7)
Z_STEPS = sum(d << (3 * i) for i, d in enumerate(Z_ORDER))
SELF = Z_ORDER.index(0)
PIECES = 8
VMEM = 62148608


def body(
    anchor_hbm, delta_hbm, scale_hbm, slot_hbm, recv_hbm, q_hbm, kv_hbm,
    cache_out, att_v,
    anchor_v, delta_v, scale_v, slot_ref, recv_ref, q_v, kv_v, stage, spread, bias_v, inv_v, inv_ref,
    perm, qf, qsend, qarr, kvsend, kvarr, send, arr,
    flat, keys, values, acc, top, outsend, outarr,
    load_sem, send_sem, recv_sem, turn_send, turn_recv, back_send, back_recv, inv_sem, out_sem, gate,
):
    store = lax.axis_index("store")
    x = lax.axis_index("tp")
    z, y, core = store // (NY * NC), (store // NC) % NY, store % NC

    loads = [
        pltpu.make_async_copy(src, dst, load_sem.at[i])
        for i, (src, dst) in enumerate(
            (
                (scale_hbm, scale_v), (slot_hbm, slot_ref), (anchor_hbm, anchor_v),
                (delta_hbm, delta_v), (q_hbm, q_v), (kv_hbm, kv_v), (recv_hbm, recv_ref),
            )
        )
    ]
    for load in loads[:4]:
        load.start()

    barrier = pltpu.get_barrier_semaphore()

    def on_line(n):
        z2, core2 = (z + (n >> 1)) & (NZ - 1), (core + (n & 1)) & (NC - 1)
        return ((z2 * NY + y) * NC + core2, x)

    def in_group(n):
        y2, x2 = (y + (n >> 2)) & (NY - 1), (x + (n & 3)) & (NX - 1)
        return ((z * NY + y2) * NC + core, x2)

    for n in range(1, 16):
        pl.semaphore_signal(barrier, inc=1, device_id=on_line(n), device_id_type=MESH)
        pl.semaphore_signal(barrier, inc=1, device_id=in_group(n), device_id_type=MESH)

    out_row = lax.broadcasted_iota(jnp.int32, (64, 64), 0)
    in_row = lax.broadcasted_iota(jnp.int32, (64, 64), 1)
    wanted = ((out_row >> 1) & 7) * 8 + (out_row >> 4) * 2 + (out_row & 1)
    perm[...] = jnp.where(in_row == wanted, 1.0, 0.0).astype(jnp.bfloat16)

    def split(tiles):
        wide = jnp.concatenate(tiles, axis=1).astype(jnp.bfloat16)
        return jnp.dot(perm[...], wide, preferred_element_type=jnp.float32).astype(jnp.bfloat16)

    loads[0].wait()
    scale = scale_v[...].astype(jnp.float32)
    slots = scale.shape[2]
    for kv in range(2):
        flat[kv * 8 : kv * 8 + 8, :] = scale[:, kv, :HD]
        flat[16 + kv * 8 : 24 + kv * 8, :] = scale[:, kv, HD : 2 * HD]
        flat[32 + kv * 8 : 40 + kv * 8, : slots - 2 * HD] = scale[:, kv, 2 * HD :]
    for slot in range(slots):
        part, lane = slot // HD * 16, slot % HD
        for kv in range(2):
            column = flat[part + kv * 8 : part + kv * 8 + 8, lane : lane + 1]
            spread[kv, slot] = jnp.broadcast_to(column, (8, HD))

    pl.semaphore_wait(barrier, 30)
    for n in range(1, 16):
        pl.semaphore_signal(gate, inc=1, device_id=in_group(n), device_id_type=MESH)

    def turn_copies(d):
        to = lax.rem(x + d, NX)
        return (
            pltpu.make_async_remote_copy(
                qsend.at[to], qarr.at[x], turn_send.at[0, d - 1], turn_recv.at[0, d - 1],
                device_id=(store, to), device_id_type=MESH,
            ),
            pltpu.make_async_remote_copy(
                kvsend.at[to], kvarr.at[x], turn_send.at[1, d - 1], turn_recv.at[1, d - 1],
                device_id=(store, to), device_id_type=MESH,
            ),
        )

    for load in loads[1:4]:
        load.wait()
    for load in loads[4:]:
        load.start()

    def offsets(j):
        return (Y_STEPS >> (2 * j)) & (NY - 1), (C_STEPS >> j) & (NC - 1)

    def z_offset(i):
        return (Z_STEPS >> (3 * i)) & (NZ - 1)

    def target(k):
        j, i = k >> 3, k & 7
        dy, dc = offsets(j)
        z2, y2, core2 = (z + z_offset(i)) & (NZ - 1), (y + dy) & (NY - 1), (core + dc) & (NC - 1)
        return (z2 * NY + y2) * NC + core2

    mine = (y * NC + core) * PER_STEP + z * NX + x

    def block_copy(k, d):
        to = (x + d) & (NX - 1)
        box = (k >> 3) + jnp.where(k >= (PLANES - 1) * NZ + NZ * 3 // 4, 1, 0)
        return pltpu.make_async_remote_copy(
            send.at[k, to], arr.at[pl.ds(mine * CAP, CAP)], send_sem.at[k >> 3], recv_sem.at[box],
            device_id=(target(k), to), device_id_type=MESH,
        )

    def decode(k):
        session = target(k)
        tiles = []
        for c in range(CAP):
            slot = jnp.maximum(slot_ref[c, 0, session], 0)
            key_scale, value_scale = spread[0, slot], spread[1, slot]
            anchor = anchor_v[slot].astype(jnp.float32)
            parts = []
            for r in range(BLK):
                delta = delta_v[slot, r].astype(jnp.float32)
                parts.append(anchor[:, :HD] + key_scale * delta[:, :HD])
                parts.append(anchor[:, HD:] + value_scale * delta[:, HD:])
            tiles.append(jnp.concatenate(parts, axis=0))
        mixed = split(tiles)
        for t in range(NX):
            for c in range(CAP):
                send[k, t, c] = mixed[t * 16 : (t + 1) * 16, c * HD : (c + 1) * HD]

    def send_line(k, _):
        decode(k)
        pl.when(k != SELF)(block_copy(k, 0).start)
        return 0

    def send_rest(k, _):
        for d in range(1, NX):
            block_copy(k, d).start()
        return 0

    def send_all(k, _):
        decode(k)
        for d in range(NX):
            block_copy(k, d).start()
        return 0

    lax.fori_loop(0, 2 * NZ, send_line, 0, unroll=4)
    arr[pl.ds(mine * CAP, CAP)] = send[SELF, x]
    pl.semaphore_wait(gate, 15)
    lax.fori_loop(0, 2 * NZ, send_rest, 0)
    loads[4].wait()
    for q in range(QPG):
        lanes = q_v[:, :, q * HD : (q + 1) * HD].astype(jnp.float32)
        qf[q] = lanes.reshape(TOK * 8, HD)
        for h in range(8):
            rows = qf[q, pl.ds(h, TOK, stride=8), :]
            qsend[h // 2, h % 2, q * TOK : (q + 1) * TOK, :] = rows.astype(jnp.bfloat16)
    loads[5].wait()
    turn_blocks = []
    for b in range(TOK // BLK):
        parts = []
        for r in range(BLK):
            row = kv_v[b * BLK + r].astype(jnp.float32)
            parts += [row[:, :HD], row[:, HD:]]
        turn_blocks.append(jnp.concatenate(parts, axis=0))
    mixed = split(turn_blocks)
    for t in range(NX):
        for b in range(TOK // BLK):
            kvsend[t, b] = mixed[t * 16 : (t + 1) * 16, b * HD : (b + 1) * HD]
    for d in range(1, NX):
        for copy in turn_copies(d):
            copy.start()
    qarr[x] = qsend[x]
    kvarr[x] = kvsend[x]
    lax.fori_loop(2 * NZ, PLANES * NZ, send_all, 0, unroll=4)
    loads[6].wait()

    recv_rows = [recv_ref[c] for c in range(CAP)]
    dead = [jnp.where(row >= 0, 0.0, 1.0) for row in recv_rows]
    dead = jnp.concatenate(dead + [jnp.zeros((8 - CAP, PER_STEP * PLANES), jnp.float32)], axis=0)
    dead = dead.astype(jnp.bfloat16)
    holder = lax.broadcasted_iota(jnp.int32, (PER_STEP * PLANES, HD), 0)
    lane = lax.broadcasted_iota(jnp.int32, (PER_STEP * PLANES, HD), 1)
    line = jnp.zeros_like(lane)
    for i, dz in enumerate(Z_ORDER):
        line = jnp.where((lane >> 4) == i, ((z - dz) & (NZ - 1)) * PER_STEP, line)
    line = line + ((lane >> 2) & 3)

    def origin(j):
        dy, dc = offsets(j)
        return ((y - dy) & (NY - 1)) * NC + ((core - dc) & (NC - 1))

    def mark(j, _):
        pick = jnp.where(holder == line + origin(j) * NX, 1.0, 0.0).astype(jnp.bfloat16)
        bias_v[j] = jnp.dot(dead, pick, preferred_element_type=jnp.float32) * LOW
        return 0

    lax.fori_loop(0, PLANES, mark, 0)

    columns = jnp.concatenate(
        recv_rows + [jnp.full((8 - CAP, PER_STEP * PLANES), -1, jnp.int32)], axis=0
    ).T
    holder = lax.broadcasted_iota(jnp.int32, (PER_STEP * PLANES, 1), 0)
    place_of = (((holder >> 2) & 7) * PER_STEP + (holder >> 5) * NX + (holder & 3)) * CAP
    for part in range(NBLK // HD):
        block = lax.broadcasted_iota(jnp.int32, (PER_STEP * PLANES, HD), 1) + part * HD
        found = jnp.zeros((PER_STEP * PLANES, HD), jnp.int32)
        for c in range(CAP):
            found = jnp.maximum(found, jnp.where(columns[:, c : c + 1] == block, place_of + c, 0))
        inv_v[part : part + 1, :] = jnp.max(found, axis=0, keepdims=True)
    inv_copy = pltpu.make_async_copy(inv_v, inv_ref, inv_sem)
    inv_copy.start()

    for d in range(1, NX):
        for copy in turn_copies(d):
            copy.wait()

    ones = jnp.ones((KEYS, HD), jnp.bfloat16)
    values[0, :, HD:] = ones
    values[1, :, HD:] = ones

    def unpack(count):
        for h in range(HEADS):
            keys[h, pl.ds(0, count), :] = flat[pl.ds(h, count, stride=4), :].astype(jnp.bfloat16)
            values[h, pl.ds(0, count), :HD] = flat[pl.ds(2 + h, count, stride=4), :].astype(
                jnp.bfloat16
            )

    flat[: TURN * 4, :] = kvarr[...].reshape(TURN * 4, HD).astype(jnp.float32)
    unpack(TURN)
    token = lax.broadcasted_iota(jnp.int32, (ROWS, TURN), 0) & (TOK - 1)
    position = lax.broadcasted_iota(jnp.int32, (ROWS, TURN), 1)
    for h in range(HEADS):
        for g in range(NX):
            scores = lax.dot_general(
                qarr[g, h], keys[h, :TURN, :], (((1,), (1,)), ((), ())),
                preferred_element_type=jnp.float32,
            )
            scores = jnp.where(position <= token + g * TOK, scores * SCALE2, LOW)
            peak = jnp.max(scores, axis=1, keepdims=True)
            power = jnp.exp2(scores - peak).astype(jnp.bfloat16)
            acc[h, g] = jnp.dot(power, values[h, :TURN, :], preferred_element_type=jnp.float32)
            top[h, g] = jnp.broadcast_to(peak, (ROWS, HD))

    def receive(j, box, count, z_from, z_to):
        first = origin(j) * (PER_STEP * CAP)
        span = arr.at[pl.ds(0, count * CAP)]
        pltpu.make_async_remote_copy(
            span, span, send_sem.at[0], recv_sem.at[box],
            device_id=(store, (x + 1) & (NX - 1)), device_id_type=MESH,
        ).wait_recv()
        lines = (z_to - z_from) * NX
        for i in range(z_from, z_to):
            at = first + ((z - Z_ORDER[i]) & (NZ - 1)) * (NX * CAP)
            for n in range(NX):
                for c in range(CAP):
                    row = (c * lines + (i - z_from) * NX + n) * 16
                    flat[row : row + 16, :] = arr[at + n * CAP + c].astype(jnp.float32)
        unpack(lines * CAP * BLK)
        rows = bias_v[j]
        return jnp.concatenate(
            [rows[c : c + 1, z_from * 16 : z_to * 16] for c in range(CAP)], axis=1
        )

    def update(bias, h, g):
        scores = lax.dot_general(
            qarr[g, h], keys[h, : bias.shape[1]], (((1,), (1,)), ((), ())),
            preferred_element_type=jnp.float32,
        )
        scores = scores * SCALE2 + bias
        before = top[h, g][:, 0:1]
        peak = jnp.maximum(before, jnp.max(scores, axis=1, keepdims=True))
        power = jnp.exp2(scores - peak).astype(jnp.bfloat16)
        total = acc[h, g] * jnp.exp2(before - peak) + jnp.dot(
            power, values[h, : bias.shape[1]], preferred_element_type=jnp.float32
        )
        return total, peak

    def attend(bias):
        for h in range(HEADS):
            for g in range(NX):
                acc[h, g], peak = update(bias, h, g)
                top[h, g] = jnp.broadcast_to(peak, (ROWS, HD))

    def step(j, _):
        attend(receive(j, j, PER_STEP, 0, NZ))
        return 0

    attend(receive(0, 0, PER_STEP - 1, 0, NZ))
    lax.fori_loop(1, PLANES - 1, step, 0)
    last, cut = PLANES - 1, NZ * 3 // 4
    attend(receive(last, last, PER_STEP * 3 // 4, 0, cut))
    bias = receive(last, last + 1, PER_STEP // 4, cut, NZ)
    def back_copy(d, h):
        to = (x + d) & (NX - 1)
        return pltpu.make_async_remote_copy(
            outsend.at[to, h], outarr.at[x, h], back_send.at[d - 1, h], back_recv.at[d - 1, h],
            device_id=(store, to), device_id_type=MESH,
        )

    for d in (2, 1, 3, 0):
        g = (x + d) & (NX - 1)
        for h in range(HEADS):
            total, _ = update(bias, h, g)
            outsend[g, h] = (total[:, :HD] / total[:, HD:]).astype(jnp.bfloat16)
            if d:
                back_copy(d, h).start()
    outarr[x] = outsend[x]

    inv_copy.wait()

    def place(b, _):
        stage[b] = arr[inv_ref[b >> 7, b & (HD - 1)]]
        return 0

    many = (NBLK + TURN_TILES) // PIECES
    moves = [
        pltpu.make_async_copy(
            stage.at[pl.ds(p * many, many)], cache_out.at[pl.ds(p * many, many)], out_sem.at[p]
        )
        for p in range(PIECES)
    ]
    stage[NBLK:] = kvarr[...].reshape(TURN_TILES, 16, HD)
    for p in range(PIECES):
        end = min((p + 1) * many, NBLK)
        lax.fori_loop(p * many, end, place, 0, unroll=8)
        moves[p].start()

    for d in range(1, NX):
        for h in range(HEADS):
            back_copy(d, h).wait()
    for t in range(NX):
        for hh in range(HEADS):
            for q in range(QPG):
                qf[q, pl.ds(t * 2 + hh, TOK, stride=8), :] = outarr[
                    t, hh, q * TOK : (q + 1) * TOK, :
                ].astype(jnp.float32)
    for q in range(QPG):
        att_v[:, :, q * HD : (q + 1) * HD] = qf[q].reshape(TOK, 8, HD).astype(jnp.bfloat16)

    for move in moves:
        move.wait()
    for j in range(PLANES):
        count = PER_STEP - 1 if j == 0 else PER_STEP
        span = arr.at[pl.ds(0, count * CAP)]
        pltpu.make_async_remote_copy(
            span, span, send_sem.at[j], recv_sem.at[j],
            device_id=(store, (x + 1) & (NX - 1)), device_id_type=MESH,
        ).wait_send()


def write_out(cache_in, att_in, cache_hbm, att_hbm, sems):
    copies = (
        pltpu.make_async_copy(cache_in, cache_hbm, sems.at[0]),
        pltpu.make_async_copy(att_in, att_hbm, sems.at[1]),
    )
    for copy in copies:
        copy.start()
    for copy in copies:
        copy.wait()


def shards(slot_anchor, slot_delta, slot_scale, send_slot, recv_block, turn_queries, turn_kv):
    bf16, f32 = jnp.bfloat16, jnp.float32
    slots = slot_anchor.shape[0]
    scales = slot_scale.transpose(1, 2, 0)
    cache_shape = (NBLK + TURN_TILES, 16, HD)
    in_hbm = pl.BlockSpec(memory_space=pltpu.HBM)
    in_vmem = pl.BlockSpec(memory_space=pltpu.VMEM)
    cache, attended = pl.pallas_call(
        body,
        out_shape=(
            pltpu.VMEM(cache_shape, bf16),
            pltpu.VMEM(turn_queries.shape, bf16),
        ),
        in_specs=[
            in_hbm, in_hbm, in_hbm, in_hbm, in_hbm, in_hbm, in_hbm,
        ],
        out_specs=(pl.BlockSpec(memory_space=pltpu.VMEM), pl.BlockSpec(memory_space=pltpu.VMEM)),
        scratch_shapes=[
            pltpu.VMEM(slot_anchor.shape, bf16),
            pltpu.VMEM(slot_delta.shape, bf16),
            pltpu.VMEM(scales.shape, bf16),
            pltpu.SMEM((CAP, 1, PLANES * NZ), jnp.int32),
            pltpu.VMEM((CAP, 1, PLANES * PER_STEP), jnp.int32),
            pltpu.VMEM(turn_queries.shape, bf16),
            pltpu.VMEM(turn_kv.shape, bf16),
            pltpu.VMEM(cache_shape, bf16),
            pltpu.VMEM((2, slots, 8, HD), f32),
            pltpu.VMEM((PLANES, 8, HD), f32),
            pltpu.VMEM((8, HD), jnp.int32),
            pltpu.SMEM((8, HD), jnp.int32),
            pltpu.VMEM((64, 64), bf16),
            pltpu.VMEM((QPG, TOK * 8, HD), f32),
            pltpu.VMEM((NX, HEADS, ROWS, HD), bf16),
            pltpu.VMEM((NX, HEADS, ROWS, HD), bf16),
            pltpu.VMEM((NX, TOK // BLK, 16, HD), bf16),
            pltpu.VMEM((NX, TOK // BLK, 16, HD), bf16),
            pltpu.VMEM((PLANES * NZ, NX, CAP, 16, HD), bf16),
            pltpu.VMEM((PLANES * PER_STEP * CAP, 16, HD), bf16),
            pltpu.VMEM((KEYS * 4, HD), f32),
            pltpu.VMEM((HEADS, KEYS, HD), bf16),
            pltpu.VMEM((HEADS, KEYS, 2 * HD), bf16),
            pltpu.VMEM((HEADS, NX, ROWS, 2 * HD), f32),
            pltpu.VMEM((HEADS, NX, ROWS, HD), f32),
            pltpu.VMEM((NX, HEADS, ROWS, HD), bf16),
            pltpu.VMEM((NX, HEADS, ROWS, HD), bf16),
            pltpu.SemaphoreType.DMA((7,)),
            pltpu.SemaphoreType.DMA((PLANES,)),
            pltpu.SemaphoreType.DMA((PLANES + 1,)),
            pltpu.SemaphoreType.DMA((2, NX - 1)),
            pltpu.SemaphoreType.DMA((2, NX - 1)),
            pltpu.SemaphoreType.DMA((NX - 1, HEADS)),
            pltpu.SemaphoreType.DMA((NX - 1, HEADS)),
            pltpu.SemaphoreType.DMA,
            pltpu.SemaphoreType.DMA((PIECES,)),
            pltpu.SemaphoreType.REGULAR,
        ],
        compiler_params=pltpu.CompilerParams(
            collective_id=0, has_side_effects=True, vmem_limit_bytes=VMEM
        ),
        name="restore_attend",
    )(
        slot_anchor, slot_delta, scales, send_slot.transpose(2, 0, 1),
        recv_block.transpose(2, 0, 1), turn_queries, turn_kv,
    )
    cache, attended = pl.pallas_call(
        write_out,
        out_shape=(
            jax.ShapeDtypeStruct(cache_shape, bf16),
            jax.ShapeDtypeStruct(turn_queries.shape, bf16),
        ),
        in_specs=[in_vmem, in_vmem],
        out_specs=(in_hbm, in_hbm),
        scratch_shapes=[pltpu.SemaphoreType.DMA((2,))],
        compiler_params=pltpu.CompilerParams(vmem_limit_bytes=2**20),
        name="write_out",
    )(cache, attended)
    cache = cache.reshape(NBLK + TURN_TILES, BLK, 2, HEADS, HD).transpose(0, 1, 3, 2, 4)
    return cache.reshape(1, (NBLK + TURN_TILES) * BLK, HEADS, 2 * HD), attended


def solution(mesh):
    placed = (
        P(("store", "tp"), None, None),
        P(("store", "tp"), None, None, None),
        P(("store", "tp"), None, None),
        P(("store", "tp"), None, None),
        P("store", None, None),
        P(("store", "tp"), None, None),
        P(("store", "tp"), None, None),
    )
    return jax.shard_map(
        shards,
        mesh=mesh,
        in_specs=placed,
        out_specs=(P("store", None, "tp", None), P(("store", "tp"), None, None)),
        check_vma=False,
    )
```
